256 devices in a mesh: col: 64 (over y, z, core), tok: 4 (over x).
Axes of the slice: x: 4, y: 4, z: 8, core: 2. Of those that a mesh axis runs over, the one named last changes fastest.
Arguments:
- krylov_basis: bfloat16 [8, 8192, 8192], P(None, 'tok', 'col'), as said below
- hessian_product: float32 [8192, 8192], P('tok', 'col'), as said below
- output_grads: bfloat16 [4096, 8192], P('col', 'tok'), may hold values from -0.26367188 to 0.26367188
- layer_inputs: bfloat16 [4096, 8192], P('tok', 'col'), may hold values from -6 to 6
- rotation: float32 [8, 4], replicated, may hold values from -3 to 3
Outputs:
- new_vector: bfloat16 [8192, 8192], P('tok', 'col')
- hessenberg: float32 [9], replicated
- influence: float32 [8, 4], replicated
The draws below stay inside these ranges and needn't reach their ends.
Inputs may be any that keep to these rules, and one draw needn't show every extreme that they name: `krylov_basis`: entries of order 1 / 8192. `hessian_product`: entries of order 1 / 8192.
All inputs are finite; a program needn't handle non-finite values.
Results may differ from the reference program's by a relative error of at most 0.005.
Values may be sent and summed in bfloat16 or wider, within the bound.
No kernel may reach another device: no remote copies, remote signals or barrier semaphores. Data moves between devices by JAX's collectives and lax.ppermute only.
A program may use at most 128 MiB of HBM per device.

```python
import jax
import jax.numpy as jnp
from jax import lax

D = 8192
K = 8
TOP = 4
LEN = 512
SEQS = 8
TOKENS = 4096


def shared_basis(key, low, high):
    key_own, key_common, key_weight = jax.random.split(key, 3)
    own = jax.random.normal(key_own, (K, D, D), jnp.float32) / D
    common = jax.random.normal(key_common, (D, D), jnp.float32) / D
    weights = jax.random.uniform(key_weight, (K,), jnp.float32, low, high)
    return own + weights[:, None, None] * common[None, :, :]


def draw_krylov_basis(key, part):
    low, high = (0.1, 0.3)
    return shared_basis(key, low, high).astype(jnp.bfloat16)


def draw_hessian_product(key, part):
    low, high = (0.1, 0.3)
    stack = shared_basis(key, low, high)
    key = jax.random.fold_in(key, 7)
    key_mix, key_noise = jax.random.split(key, 2)
    mixing = jax.random.uniform(key_mix, (K,), jnp.float32, 0.5, 2.0)
    mixed = jnp.tensordot(mixing, stack, axes=1)
    noise = jax.random.normal(key_noise, (D, D), jnp.float32) * 0.6 / D
    return mixed + noise


def block_levels(rng, extent, shards, smallest, high):
    level = 1.0
    for axis_at, shards_of in shards:
        heights = jax.random.uniform(jax.random.fold_in(jax.random.fold_in(rng, 6), axis_at), (shards_of,), jnp.float32, smallest / len(shards), high / len(shards))
        level = level * jnp.repeat(jnp.exp(heights), extent[axis_at] // shards_of).reshape((-1,) + (1,) * (len(extent) - 1 - axis_at))
    return level


def centred(stream_key, dims, spread, most, cuts=(), held_as=jnp.bfloat16):
    loudness = block_levels(stream_key, dims, cuts, -0.22, 0.18) if cuts else 1.0
    values = jax.random.normal(stream_key, dims, jnp.float32) * spread * loudness
    return jnp.minimum(jnp.maximum(values, -most), most).astype(held_as)


def setup_inputs(seed: int = 0) -> dict:
    seeds = jax.random.split(jax.random.key(seed), 6)
    return {
        "krylov_basis": draw_krylov_basis(jax.random.fold_in(seeds[5], 71), 0),
        "hessian_product": draw_hessian_product(jax.random.fold_in(seeds[5], 71), 0),
        "output_grads": centred(seeds[2], (TOKENS, D), (1.0 / LEN ** 0.5), 0.26367188, ((0, 64), (1, 4))),
        "layer_inputs": centred(seeds[3], (TOKENS, D), 1.0, 6.0, ((0, 4), (1, 64))),
        "rotation": centred(seeds[4], (K, TOP), 0.5, 3.0, (), jnp.float32),
    }


def inner_all(stack, field):
    return lax.map(lambda matrix: jnp.sum(matrix.astype(jnp.float32) * field), stack)

def remove_all(field, weights, stack):

    def advance(carry, pair):
        weight, matrix = pair
        return (carry - weight * matrix.astype(jnp.float32), None)
    return lax.scan(advance, field, (weights, stack))[0]

def reference(krylov_basis, hessian_product, output_grads, layer_inputs, rotation):
    first_dots = inner_all(krylov_basis, hessian_product)
    remainder = remove_all(hessian_product, first_dots, krylov_basis)
    second_dots = inner_all(krylov_basis, remainder)
    remainder = remove_all(remainder, second_dots, krylov_basis)
    length = jnp.sqrt(jnp.sum(remainder * remainder) + 1e-06)
    new_vector = (remainder / length).astype(jnp.bfloat16)
    hessenberg = jnp.concatenate([first_dots + second_dots, length[None]])

    def example(index):
        start = (index * LEN).astype(jnp.int32)
        grad_part = lax.dynamic_slice_in_dim(output_grads, start, LEN, 0)
        input_part = lax.dynamic_slice_in_dim(layer_inputs, start, LEN, 0)
        tile = jnp.dot(grad_part.T, input_part, preferred_element_type=jnp.float32)
        return inner_all(krylov_basis, tile)
    coordinates = lax.map(example, jnp.arange(SEQS, dtype=jnp.int32))
    influence = jnp.dot(coordinates, rotation, precision=lax.Precision.HIGHEST)
    return (new_vector, hessenberg, influence)
```

```python
import functools

import jax
import jax.numpy as jnp
from jax import lax
from jax.experimental import pallas as pl
from jax.experimental.pallas import tpu as pltpu
from jax.sharding import PartitionSpec as P

LEN = 512
SEQS = 8
K = 8
TOP = 4
YS = 4
ZS = 8
XS = 4
CHIP = 128
PAIRS = [(k, l) for k in range(K) for l in range(k, K)]
HIGHEST = lax.Precision.HIGHEST
MB = 2**20


def index_of(y, z, core):
    return ((y % YS) * ZS + z % ZS) * 2 + core


def shift_yz(value, dy, dz):
    pairs = [
        (index_of(y, z, c), index_of(y + dy, z + dz, c))
        for y in range(YS)
        for z in range(ZS)
        for c in range(2)
    ]
    return lax.ppermute(value, "col", pairs)


def shift_x(value, dx):
    return lax.ppermute(value, "tok", [(x, (x + dx) % XS) for x in range(XS)])


def swap_core(value):
    return lax.ppermute(value, "col", [(i, i ^ 1) for i in range(2 * YS * ZS)])


def sum_everywhere(value):
    value = value + shift_yz(value, 0, 1) + shift_yz(value, 0, -1) + shift_yz(value, 0, 2)
    value = value + shift_yz(value, 0, 4)
    value = value + shift_yz(value, 1, 0) + shift_yz(value, 2, 0) + shift_yz(value, -1, 0)
    value = value + shift_x(value, 1) + shift_x(value, 2) + shift_x(value, -1)
    return value + swap_core(value)


def lane_sums(rows):
    return lax.dot_general(
        jnp.ones((8, 128), jnp.float32),
        rows,
        (((1,), (1,)), ((), ())),
        precision=HIGHEST,
        preferred_element_type=jnp.float32,
    )


def gram_kernel(basis_ref, field_ref, out_ref, rows_ref):
    count = len(PAIRS) + K

    def step(at, totals):
        rows = pl.ds(pl.multiple_of(at * 16, 16), 16)
        stack = [basis_ref[k, rows, :].astype(jnp.float32) for k in range(K)]
        field = field_ref[rows, :]
        terms = [stack[k] * stack[l] for k, l in PAIRS] + [stack[k] * field for k in range(K)]
        return tuple(t + (a[:8] + a[8:]) for t, a in zip(totals, terms))

    zero = jnp.zeros((8, 128), jnp.float32)
    totals = lax.fori_loop(0, field_ref.shape[0] // 16, step, (zero,) * count)
    rows_ref[...] = jnp.zeros_like(rows_ref)
    for at, total in enumerate(totals):
        rows_ref[at : at + 1, :] = jnp.sum(total, axis=0, keepdims=True)
    out_ref[...] = lane_sums(rows_ref[...])


def gram(basis, field):
    return pl.pallas_call(
        gram_kernel,
        out_shape=jax.ShapeDtypeStruct((8, 128), jnp.float32),
        in_specs=[pl.BlockSpec(memory_space=pltpu.VMEM)] * 2,
        out_specs=pl.BlockSpec(memory_space=pltpu.VMEM),
        scratch_shapes=[pltpu.VMEM((128, 128), jnp.float32)],
        compiler_params=pltpu.CompilerParams(vmem_limit_bytes=16 * MB),
        cost_estimate=pl.CostEstimate(flops=24 * MB, bytes_accessed=5 * MB, transcendentals=0),
        name="gram",
    )(basis, field)


def remainder_kernel(dots_ref, basis_ref, field_ref, rest_ref, squares_ref, weights_ref):
    first = [dots_ref[0, len(PAIRS) + k] for k in range(K)]
    weights = []
    for k in range(K):
        overlap = first[0] * dots_ref[0, PAIRS.index((0, k))]
        for l in range(1, K):
            overlap += first[l] * dots_ref[0, PAIRS.index((min(k, l), max(k, l)))]
        weights.append(first[k] + (first[k] - overlap))
    lane = lax.broadcasted_iota(jnp.int32, (8, 128), 1)
    row = jnp.zeros((8, 128), jnp.float32)
    for k in range(K):
        row = jnp.where(lane == k, weights[k], row)
    weights_ref[...] = row

    def step(at, total):
        rows = pl.ds(pl.multiple_of(at * 16, 16), 16)
        rest = field_ref[rows, :]
        for k in range(K):
            rest = rest - weights[k] * basis_ref[k, rows, :].astype(jnp.float32)
        rest_ref[rows, :] = rest
        square = rest * rest
        return total + (square[:8] + square[8:])

    squares_ref[...] = lax.fori_loop(
        0, field_ref.shape[0] // 16, step, jnp.zeros((8, 128), jnp.float32)
    )


def remainder(dots, basis, field):
    vmem = pl.BlockSpec(memory_space=pltpu.VMEM)
    small = jax.ShapeDtypeStruct((8, 128), jnp.float32)
    return pl.pallas_call(
        remainder_kernel,
        out_shape=[jax.ShapeDtypeStruct(field.shape, jnp.float32), small, small],
        in_specs=[pl.BlockSpec(memory_space=pltpu.SMEM), vmem, vmem],
        out_specs=[vmem, vmem, vmem],
        compiler_params=pltpu.CompilerParams(vmem_limit_bytes=16 * MB),
        cost_estimate=pl.CostEstimate(flops=6 * MB, bytes_accessed=6 * MB, transcendentals=0),
        name="remainder",
    )(dots, basis, field)


def turn_basis_kernel(core_ref, own_ref, other_ref, out_ref):
    out_ref[0, :128, :] = own_ref[0].T
    out_ref[0, 128:, :] = other_ref[0].T


def turn_basis(core, basis, other):
    half = other.shape[1]
    return pl.pallas_call(
        turn_basis_kernel,
        out_shape=jax.ShapeDtypeStruct((K, 256, half), jnp.bfloat16),
        grid_spec=pltpu.PrefetchScalarGridSpec(
            num_scalar_prefetch=1,
            grid=(K,),
            in_specs=[
                pl.BlockSpec((1, half, 128), lambda k, core: (k, core[0], 0)),
                pl.BlockSpec((1, half, 128), lambda k, core: (k, 0, 0)),
            ],
            out_specs=pl.BlockSpec((1, 256, half), lambda k, core: (k, 0, 0)),
        ),
        compiler_params=pltpu.CompilerParams(vmem_limit_bytes=16 * MB),
        cost_estimate=pl.CostEstimate(flops=0, bytes_accessed=8 * MB, transcendentals=0),
        name="turn_basis",
    )(core, basis, other)


def turn_inputs_kernel(own_ref, other_ref, out_ref):
    out_ref[:128, :] = own_ref[...].T
    out_ref[128:, :] = other_ref[...].T


def turn_inputs(own, other):
    tokens = own.shape[0]
    return pl.pallas_call(
        turn_inputs_kernel,
        out_shape=jax.ShapeDtypeStruct((256, tokens), jnp.bfloat16),
        grid=(4,),
        in_specs=[pl.BlockSpec((tokens // 4, 128), lambda t: (t, 0))] * 2,
        out_specs=pl.BlockSpec((256, tokens // 4), lambda t: (0, t)),
        compiler_params=pltpu.CompilerParams(vmem_limit_bytes=16 * MB),
        cost_estimate=pl.CostEstimate(flops=0, bytes_accessed=4 * MB, transcendentals=0),
        name="turn_inputs",
    )(own, other)


def project_kernel(place_ref, inputs_ref, a_ref, b_ref, basis_ref, squares_ref, out_ref, rows_ref, tile_ref):
    s = pl.program_id(0)
    y, z = place_ref[0], place_ref[1]
    dy = lax.rem(y - s // 2 + YS, YS)
    first_z = lax.rem(s, 2) * 4
    wide = a_ref.shape[-1]

    @pl.when(s == 0)
    def _():
        rows_ref[...] = jnp.zeros_like(rows_ref)
        rows_ref[64:65, :] = jnp.sum(squares_ref[...], axis=0, keepdims=True)

    for part in range(2):
        tile = None
        for j in range(4):
            dz = lax.rem(z - first_z - j + ZS, ZS)
            grads = a_ref[dz, dy] if part == 0 else b_ref[dy, dz]
            term = jnp.dot(
                inputs_ref[:, j * CHIP : (j + 1) * CHIP], grads, preferred_element_type=jnp.float32
            )
            tile = term if tile is None else tile + term
        tile_ref[:, part * wide : (part + 1) * wide] = tile

    def step(at, totals):
        rows = pl.ds(pl.multiple_of(at * 16, 16), 16)
        totals = list(totals)
        for c in range(2 * wide // 128):
            cols = slice(c * 128, (c + 1) * 128)
            tile = tile_ref[rows, cols]
            for k in range(K):
                term = tile * basis_ref[k, rows, cols].astype(jnp.float32)
                totals[k] = totals[k] + (term[:8] + term[8:])
        return tuple(totals)

    totals = lax.fori_loop(0, 16, step, (jnp.zeros((8, 128), jnp.float32),) * K)
    sums = jnp.concatenate([jnp.sum(t, axis=0, keepdims=True) for t in totals], axis=0)
    rows_ref[pl.ds(pl.multiple_of(s * K, K), K), :] = sums

    @pl.when(s == SEQS - 1)
    def _():
        out_ref[...] = lane_sums(rows_ref[...])


def project(place, inputs, a, b, basis, squares):
    wide = a.shape[-1]
    vmem = pl.BlockSpec(memory_space=pltpu.VMEM)
    return pl.pallas_call(
        project_kernel,
        out_shape=jax.ShapeDtypeStruct((8, 128), jnp.float32),
        grid_spec=pltpu.PrefetchScalarGridSpec(
            num_scalar_prefetch=1,
            grid=(SEQS,),
            in_specs=[pl.BlockSpec((256, LEN), lambda s, place: (0, s)), vmem, vmem, vmem, vmem],
            out_specs=pl.BlockSpec((8, 128), lambda s, place: (0, 0)),
            scratch_shapes=[
                pltpu.VMEM((128, 128), jnp.float32),
                pltpu.VMEM((256, 2 * wide), jnp.float32),
            ],
        ),
        compiler_params=pltpu.CompilerParams(vmem_limit_bytes=32 * MB),
        cost_estimate=pl.CostEstimate(
            flops=4500 * MB, bytes_accessed=14 * MB, transcendentals=0
        ),
        name="project",
    )(place, inputs, a, b, basis, squares)


def finish_kernel(sums_ref, weights_ref, spread_ref, rest_ref, new_ref, hessenberg_ref, influence_ref):
    sums = sums_ref[...]
    length = jnp.sqrt(sums[0:1, 64:65] + 1e-06)
    new_ref[...] = (rest_ref[...] / length).astype(jnp.bfloat16)
    lane = lax.broadcasted_iota(jnp.int32, (8, 128), 1)
    row = lax.broadcasted_iota(jnp.int32, (8, 128), 0)
    hessenberg_ref[...] = jnp.where(lane == K, length, weights_ref[...])[0:1, : K + 1]
    mine = jnp.where(lane // K == row, sums, 0.0)
    influence_ref[...] = jnp.dot(
        mine, spread_ref[...], precision=HIGHEST, preferred_element_type=jnp.float32
    )[:, :TOP]


def finish(sums, weights, spread, rest):
    vmem = pl.BlockSpec(memory_space=pltpu.VMEM)
    return pl.pallas_call(
        finish_kernel,
        out_shape=[
            jax.ShapeDtypeStruct(rest.shape, jnp.bfloat16),
            jax.ShapeDtypeStruct((1, K + 1), jnp.float32),
            jax.ShapeDtypeStruct((SEQS, TOP), jnp.float32),
        ],
        in_specs=[vmem] * 4,
        out_specs=[vmem] * 3,
        compiler_params=pltpu.CompilerParams(vmem_limit_bytes=16 * MB),
        cost_estimate=pl.CostEstimate(flops=MB, bytes_accessed=2 * MB, transcendentals=0),
        name="finish",
    )(sums, weights, spread, rest)


def gather_grads(piece):
    half = piece.shape[1] // 2
    a, b = piece[:, :half], piece[:, half:]
    a1, a3 = shift_yz(a, 1, 0), shift_yz(a, -1, 0)
    a2 = jnp.concatenate([shift_yz(a1[:64], 1, 0), shift_yz(a3[64:], -1, 0)])
    b1, b7 = shift_yz(b, 0, 1), shift_yz(b, 0, -1)
    b2, b6 = shift_yz(b1, 0, 1), shift_yz(b7, 0, -1)
    b3, b5 = shift_yz(b2, 0, 1), shift_yz(b6, 0, -1)
    b4 = jnp.concatenate([shift_yz(b3[:64], 0, 1), shift_yz(b5[64:], 0, -1)])
    aa = jnp.concatenate([a, a1, a2, a3])
    bb = jnp.concatenate([b, b1, b2, b3, b4, b5, b6, b7])
    u1, u7 = shift_yz(aa, 0, 1), shift_yz(aa, 0, -1)
    u2, u6 = shift_yz(u1, 0, 1), shift_yz(u7, 0, -1)
    u3, u5 = shift_yz(u2, 0, 1), shift_yz(u6, 0, -1)
    u4 = jnp.concatenate([shift_yz(u3[:256], 0, 1), shift_yz(u5[256:], 0, -1)])
    w1, w3 = shift_yz(bb, 1, 0), shift_yz(bb, -1, 0)
    w2 = jnp.concatenate([shift_yz(w1[:512], 1, 0), shift_yz(w3[512:], -1, 0)])
    left = jnp.stack([aa, u1, u2, u3, u4, u5, u6, u7]).reshape(ZS, YS, CHIP, half)
    right = jnp.stack([bb, w1, w2, w3]).reshape(YS, ZS, CHIP, half)
    return left, right


def on_device(krylov_basis, hessian_product, output_grads, layer_inputs, rotation):
    col = lax.axis_index("col")
    core = lax.rem(col, 2)
    place = jnp.stack([col // (2 * ZS), lax.rem(col // 2, ZS)]).astype(jnp.int32)
    half = krylov_basis.shape[1] // 2
    rows = output_grads.shape[0]

    kept = lax.dynamic_slice_in_dim(output_grads, core * half, half, 1)
    given = swap_core(lax.dynamic_slice_in_dim(output_grads, (1 - core) * half, half, 1))
    piece = jnp.zeros((2 * rows, half), output_grads.dtype)
    piece = lax.dynamic_update_slice_in_dim(piece, kept, core * rows, 0)
    piece = lax.dynamic_update_slice_in_dim(piece, given, (1 - core) * rows, 0)
    left, right = gather_grads(piece)

    other_basis = swap_core(
        lax.dynamic_slice_in_dim(krylov_basis, (1 - core) * half, half, 1)
    )
    basis = turn_basis(core[None].astype(jnp.int32), krylov_basis, other_basis)

    own_inputs = lax.all_gather(layer_inputs, "tok", axis=0, tiled=True)
    inputs = turn_inputs(own_inputs, swap_core(own_inputs))

    dots = sum_everywhere(gram(krylov_basis, hessian_product))
    rest, squares, weights = remainder(dots, krylov_basis, hessian_product)

    sums = sum_everywhere(project(place, inputs, left, right, basis, squares))
    spread = jnp.pad(jnp.tile(rotation, (SEQS, 1)), ((0, 128 - SEQS * K), (0, 128 - TOP)))
    new_vector, hessenberg, influence = finish(sums, weights, spread, rest)
    return new_vector, hessenberg[0], influence


def solution(mesh):
    return jax.shard_map(
        on_device,
        mesh=mesh,
        in_specs=(P(None, "tok", "col"), P("tok", "col"), P("col", "tok"), P("tok", "col"), P()),
        out_specs=(P("tok", "col"), P(), P()),
        check_vma=False,
    )
```

```python
import functools

import jax
import jax.numpy as jnp
from jax import lax
from jax.experimental import pallas as pl
from jax.experimental.pallas import tpu as pltpu
from jax.sharding import PartitionSpec as P

LEN = 512
SEQS = 8
K = 8
TOP = 4
YS = 4
ZS = 8
XS = 4
CHIP = 128
WIDE = 512
FIRST = 16
PAIRS = [(k, l) for k in range(K) for l in range(k, K)]
HIGHEST = lax.Precision.HIGHEST
MB = 2**20


def toward(value, axis, sign):
    size = lax.axis_size(axis)
    axes = ("core", axis) if axis == "x" else (axis, "core")

    def place(i, core):
        return core * size + i if axis == "x" else i * 2 + core

    pairs = [
        (place(i, core), place((i + (sign if core == 0 else -sign)) % size, core))
        for i in range(size)
        for core in range(2)
    ]
    return lax.ppermute(value, axes, pairs)


def swap_core(value):
    return lax.ppermute(value, "core", [(0, 1), (1, 0)])


def together(*values):
    return lax.optimization_barrier(values)


def sum_over(value, axes):
    copies = jnp.broadcast_to(value[None], (lax.axis_size(axes),) + value.shape)
    return jnp.sum(lax.all_to_all(copies, axes, 0, 0), axis=0)


def sum_everywhere(value):
    return sum_over(sum_over(value, ("z", "core")), ("y", "x"))


def lane_sums(rows):
    return lax.dot_general(
        jnp.ones((8, 128), jnp.float32),
        rows,
        (((1,), (1,)), ((), ())),
        precision=HIGHEST,
        preferred_element_type=jnp.float32,
    )


def gram_kernel(basis_ref, field_ref, out_ref, rows_ref):
    count = len(PAIRS) + K + 1

    def step(at, totals):
        rows = pl.ds(pl.multiple_of(at * 16, 16), 16)
        stack = [basis_ref[k, rows, :].astype(jnp.float32) for k in range(K)]
        field = field_ref[rows, :]
        terms = [stack[k] * stack[l] for k, l in PAIRS] + [stack[k] * field for k in range(K)]
        terms.append(field * field)
        return tuple(t + (a[:8] + a[8:]) for t, a in zip(totals, terms))

    zero = jnp.zeros((8, 128), jnp.float32)
    totals = lax.fori_loop(0, field_ref.shape[0] // 16, step, (zero,) * count)
    rows_ref[...] = jnp.zeros_like(rows_ref)
    for at, total in enumerate(totals):
        rows_ref[FIRST + at : FIRST + at + 1, :] = jnp.sum(total, axis=0, keepdims=True)
    sums = lane_sums(rows_ref[...])
    row = lax.broadcasted_iota(jnp.int32, (8, 128), 0)
    out_ref[...] = jnp.where(row == 0, sums, 0.0)


def gram(basis, field):
    return pl.pallas_call(
        gram_kernel,
        out_shape=jax.ShapeDtypeStruct((8, 128), jnp.float32),
        in_specs=[pl.BlockSpec(memory_space=pltpu.VMEM)] * 2,
        out_specs=pl.BlockSpec(memory_space=pltpu.VMEM),
        scratch_shapes=[pltpu.VMEM((128, 128), jnp.float32)],
        compiler_params=pltpu.CompilerParams(vmem_limit_bytes=8 * MB),
        cost_estimate=pl.CostEstimate(flops=24 * MB, bytes_accessed=18 * MB, transcendentals=0),
        name="gram",
    )(basis, field)


def weigh(sums_ref):
    def overlap(k, l):
        return sums_ref[0, FIRST + PAIRS.index((min(k, l), max(k, l)))]

    def times(vector):
        product = []
        for k in range(K):
            total = overlap(k, 0) * vector[0]
            for l in range(1, K):
                total += overlap(k, l) * vector[l]
            product.append(total)
        return product

    first = [sums_ref[0, FIRST + len(PAIRS) + k] for k in range(K)]
    whole = sums_ref[0, FIRST + len(PAIRS) + K]
    weights = [f + (f - t) for f, t in zip(first, times(first))]
    squares = whole
    for weight, dot, turned in zip(weights, first, times(weights)):
        squares += weight * (turned - (dot + dot))
    return weights, squares, whole


def take_off(weights, basis_ref, field_ref, rows):
    rest = field_ref[rows, :]
    for k in range(K):
        rest = rest - weights[k] * basis_ref[k, rows, :].astype(jnp.float32)
    return rest


def squares_kernel(sums_ref, basis_ref, field_ref, out_ref):
    weights = weigh(sums_ref)[0]

    def step(at, total):
        rest = take_off(weights, basis_ref, field_ref, pl.ds(pl.multiple_of(at * 16, 16), 16))
        square = rest * rest
        return total + (square[:8] + square[8:])

    out_ref[...] = lax.fori_loop(
        0, field_ref.shape[0] // 16, step, jnp.zeros((8, 128), jnp.float32)
    )


def squared_length(sums, basis, field):
    vmem = pl.BlockSpec(memory_space=pltpu.VMEM)
    parts = pl.pallas_call(
        squares_kernel,
        out_shape=jax.ShapeDtypeStruct((8, 128), jnp.float32),
        in_specs=[pl.BlockSpec(memory_space=pltpu.SMEM), vmem, vmem],
        out_specs=vmem,
        compiler_params=pltpu.CompilerParams(vmem_limit_bytes=8 * MB),
        name="squares",
    )(sums, basis, field)
    return jnp.sum(sum_everywhere(parts))


def finish_kernel(given, scalars_ref, squares_ref, sums_ref, rotation_ref, basis_ref, field_ref, *out_refs):
    new_ref, hessenberg_ref, influence_ref, little_ref = out_refs
    weights, squares, whole = weigh(scalars_ref)
    little_ref[0] = jnp.where(squares * 256.0 < whole, 1, 0)
    if given:
        squares = squares_ref[0]
    length = jnp.sqrt(jnp.full((16, 128), squares, jnp.float32) + 1e-06)
    scale = 1.0 / length

    def step(at, carry):
        rows = pl.ds(pl.multiple_of(at * 16, 16), 16)
        rest = take_off(weights, basis_ref, field_ref, rows)
        new_ref[rows, :] = (rest * scale).astype(jnp.bfloat16)
        return carry

    lax.fori_loop(0, field_ref.shape[0] // 16, step, 0, unroll=4)
    lane = lax.broadcasted_iota(jnp.int32, (8, 128), 1)
    row = length[:8]
    for k in range(K):
        row = jnp.where(lane == k, weights[k], row)
    hessenberg_ref[...] = row[0:1, : K + 1]
    influence_ref[...] = jnp.dot(
        jnp.where(lane < K, sums_ref[...], 0.0),
        rotation_ref[...],
        precision=HIGHEST,
        preferred_element_type=jnp.float32,
    )[:, :TOP]


def finish(given, squares, sums, rotation, basis, field):
    vmem, smem = (pl.BlockSpec(memory_space=m) for m in (pltpu.VMEM, pltpu.SMEM))
    return pl.pallas_call(
        functools.partial(finish_kernel, given),
        out_shape=[
            jax.ShapeDtypeStruct(field.shape, jnp.bfloat16),
            jax.ShapeDtypeStruct((1, K + 1), jnp.float32),
            jax.ShapeDtypeStruct((SEQS, TOP), jnp.float32),
            jax.ShapeDtypeStruct((1,), jnp.int32),
        ],
        in_specs=[smem, smem] + [vmem] * 4,
        out_specs=[vmem] * 3 + [smem],
        compiler_params=pltpu.CompilerParams(vmem_limit_bytes=8 * MB),
        cost_estimate=pl.CostEstimate(flops=6 * MB, bytes_accessed=6 * MB, transcendentals=0),
        name="finish",
    )(sums, squares, sums, rotation, basis, field)


def turn_basis_kernel(core_ref, own_ref, other_ref, out_ref):
    out_ref[0, :128, :] = own_ref[0].T
    out_ref[0, 128:, :] = other_ref[0].T


def turn_basis(core, basis, other):
    half = other.shape[1] // 2
    return pl.pallas_call(
        turn_basis_kernel,
        out_shape=jax.ShapeDtypeStruct((K, 256, half), jnp.bfloat16),
        grid_spec=pltpu.PrefetchScalarGridSpec(
            num_scalar_prefetch=1,
            grid=(K,),
            in_specs=[pl.BlockSpec((1, half, 128), lambda k, core: (k, core[0], 0))] * 2,
            out_specs=pl.BlockSpec((1, 256, half), lambda k, core: (k, 0, 0)),
        ),
        compiler_params=pltpu.CompilerParams(vmem_limit_bytes=8 * MB),
        cost_estimate=pl.CostEstimate(flops=0, bytes_accessed=8 * MB, transcendentals=0),
        name="turn_basis",
    )(core, basis, other)


def turn_inputs_kernel(core_ref, own_ref, other_ref, out_ref):
    for at, ref in enumerate((own_ref, other_ref)):
        parts = ref[...].reshape(-1, 2, CHIP // 2, 128)
        turned = jnp.concatenate([parts[:, 1:], parts[:, :1]], axis=1)
        parts = jnp.where(core_ref[0] == 1, turned, parts)
        out_ref[at * 128 : (at + 1) * 128, :] = parts.reshape(-1, 128).T


def turn_inputs(core, own, other):
    vmem = pl.BlockSpec(memory_space=pltpu.VMEM)
    return pl.pallas_call(
        turn_inputs_kernel,
        out_shape=jax.ShapeDtypeStruct((256, own.shape[0]), jnp.bfloat16),
        in_specs=[pl.BlockSpec(memory_space=pltpu.SMEM), vmem, vmem],
        out_specs=vmem,
        compiler_params=pltpu.CompilerParams(vmem_limit_bytes=8 * MB),
        cost_estimate=pl.CostEstimate(flops=0, bytes_accessed=MB, transcendentals=0),
        name="turn_inputs",
    )(core, own, other)


def keep_parts(parts_ref, slot, tile):
    high = tile.astype(jnp.bfloat16)
    parts_ref[2 * slot] = high
    parts_ref[2 * slot + 1] = (tile - high.astype(jnp.float32)).astype(jnp.bfloat16)


def products(parts_ref, count, basis_ref, first):
    def step(at, total):
        rows = pl.ds(pl.multiple_of(at * 32, 32), 32)
        tiles = parts_ref[: 2 * count, rows, :].reshape(count * 64, WIDE)
        basis = basis_ref[:, rows, first : first + WIDE].reshape(256, WIDE)
        return total + lax.dot_general(
            tiles, basis, (((1,), (1,)), ((), ())), preferred_element_type=jnp.float32
        )

    cross = lax.fori_loop(0, 8, step, jnp.zeros((count * 64, 256), jnp.float32))
    row = lax.broadcasted_iota(jnp.int32, cross.shape, 0)
    lane = lax.broadcasted_iota(jnp.int32, cross.shape, 1)
    cross = jnp.where(lax.rem(row, 32) == lax.rem(lane, 32), cross, 0.0)
    sums = jnp.sum(cross.reshape(count, 64, 256), axis=1)
    owner = lax.broadcasted_iota(jnp.int32, (256, 128), 0) // 32
    pick = (owner == lax.broadcasted_iota(jnp.int32, (256, 128), 1)).astype(jnp.float32)
    return jnp.dot(sums, pick, precision=HIGHEST, preferred_element_type=jnp.float32)


class Place:
    def __init__(self, ref):
        self.y, self.z, self.x, self.sign = (ref[i] for i in range(4))

    def y_slot(self, y):
        return lax.rem(self.sign * (self.y - y) + 2 * YS, YS)

    def z_slot(self, z):
        return lax.rem(self.sign * (self.z - z) + 2 * ZS, ZS)

    def x_slot(self, x):
        return lax.rem(self.sign * (self.x - x) + 2 * XS, XS)

    def y_of(self, slot):
        return lax.rem(self.y - self.sign * slot + 2 * YS, YS)


def chip_rows(slot):
    return pl.ds(pl.multiple_of(slot * CHIP, CHIP), CHIP)


def example_tile(place, inputs_ref, y, part, block):
    grads = jnp.concatenate([block(place.z_slot(part * 4 + j)) for j in range(4)], axis=0)
    cols = pl.ds(pl.multiple_of(part * LEN, LEN), LEN)
    inputs = inputs_ref[place.x_slot(y), :, cols]
    return jnp.dot(inputs, grads, preferred_element_type=jnp.float32)


def rows_example(place, inputs_ref, parts_ref, at, slot_y, ref):
    y = place.y_of(slot_y)
    for part in range(2):
        tile = example_tile(place, inputs_ref, y, part, lambda d: ref[chip_rows(d), :])
        keep_parts(parts_ref, at + part, tile)
    return [y * 2, y * 2 + 1]


def near_kernel(place_ref, basis_ref, before_ref, *refs):
    left, right, (out_ref, left_ref, inputs_ref, parts_ref) = refs[4:11], refs[11:14], refs[14:]
    for slot in range(XS):
        inputs_ref[slot] = refs[slot][...]
    place = Place(place_ref)
    out_ref[...] = before_ref[...]
    for slot, ref in zip((0, 1, 2, 3, 5, 6, 7), left):
        left_ref[slot] = ref[...]
    left_ref[4] = jnp.zeros_like(left_ref[4])

    def one(example, carry):
        y = example // 2
        rows = chip_rows(place.y_slot(y))
        tile = example_tile(
            place, inputs_ref, y, lax.rem(example, 2), lambda d: left_ref[d, rows, :]
        )
        keep_parts(parts_ref, example, tile)
        return carry

    lax.fori_loop(0, SEQS, one, 0)
    out_ref[...] += products(parts_ref, SEQS, basis_ref, 0)

    owners = []
    for at, (slot_y, ref) in enumerate(zip((0, 1, 3), right)):
        owners += rows_example(place, inputs_ref, parts_ref, 2 * at, slot_y, ref)
    sums = products(parts_ref, len(owners), basis_ref, WIDE)
    for at, owner in enumerate(owners):
        out_ref[pl.ds(owner, 1), :] += sums[at : at + 1]


def far_kernel(place_ref, basis_ref, before_ref, *refs):
    left_ref, right_ref, out_ref, inputs_ref, parts_ref = refs[4:]
    for slot in range(XS):
        inputs_ref[slot] = refs[slot][...]
    place = Place(place_ref)
    out_ref[...] = before_ref[...]
    z = lax.rem(place.z + 4, ZS)
    owners = []
    for slot_y in range(YS):
        y = place.y_of(slot_y)
        tile = jnp.dot(
            inputs_ref[place.x_slot(y), :, chip_rows(z)],
            left_ref[slot_y * CHIP : (slot_y + 1) * CHIP, :],
            preferred_element_type=jnp.float32,
        )
        keep_parts(parts_ref, slot_y, tile)
        owners.append(y * 2 + z // 4)
    left = products(parts_ref, YS, basis_ref, 0)
    owners += rows_example(place, inputs_ref, parts_ref, 0, 2, right_ref)
    right = products(parts_ref, 2, basis_ref, WIDE)
    for at, owner in enumerate(owners):
        row = left[at : at + 1] if at < YS else right[at - YS : at - YS + 1]
        out_ref[pl.ds(owner, 1), :] += row


def project(kernel, place, inputs, basis, before, grads, slots, scratch):
    vmem = pl.BlockSpec(memory_space=pltpu.VMEM)
    return pl.pallas_call(
        kernel,
        out_shape=jax.ShapeDtypeStruct((8, 128), jnp.float32),
        in_specs=[pl.BlockSpec(memory_space=pltpu.SMEM)] + [vmem] * (2 + len(inputs) + len(grads)),
        out_specs=vmem,
        scratch_shapes=scratch
        + [
            pltpu.VMEM((XS,) + inputs[0].shape, jnp.bfloat16),
            pltpu.VMEM((2 * slots, 256, WIDE), jnp.bfloat16),
        ],
        compiler_params=pltpu.CompilerParams(vmem_limit_bytes=16 * MB),
        cost_estimate=pl.CostEstimate(
            flops=sum(512 * g.size for g in grads) + 512 * MB * slots,
            bytes_accessed=4 * MB,
            transcendentals=0,
        ),
        name=kernel.__name__,
    )(place, basis, before, *inputs, *grads)


def on_device(krylov_basis, hessian_product, output_grads, layer_inputs, rotation):
    core = lax.axis_index("core")
    place = [lax.axis_index(axis) for axis in ("y", "z", "x")] + [1 - 2 * core]
    place = jnp.stack(place).astype(jnp.int32)
    core_id = core[None].astype(jnp.int32)
    half = krylov_basis.shape[1] // 2

    both = (output_grads, swap_core(output_grads))
    a, b = (
        jnp.concatenate(
            [lax.dynamic_slice_in_dim(g, core * half + at * WIDE, WIDE, 1) for g in both]
        )
        for at in range(2)
    )
    b1, b7 = toward(b, "z", 1), toward(b, "z", -1)
    a1, a3 = toward(a, "y", 1), toward(a, "y", -1)
    b1, krylov, layer = together(b1, krylov_basis, layer_inputs)
    x0 = turn_inputs(core_id, layer, swap_core(layer))
    x1, x3 = toward(x0, "x", 1), toward(x0, "x", -1)
    basis = turn_basis(core_id, krylov, swap_core(krylov))
    b2, b6 = toward(b1, "z", 1), toward(b7, "z", -1)
    a2 = toward(a1, "y", 1)
    l0 = jnp.concatenate([a, a1, a2, a3])
    l1, l7 = toward(l0, "z", 1), toward(l0, "z", -1)
    b3, b5 = toward(b2, "z", 1), toward(b6, "z", -1)
    b4 = toward(b3, "z", 1)
    b4, basis = together(b4, basis)
    r0 = jnp.concatenate([b, b1, b2, b3, b4, b5, b6, b7])
    x2 = toward(x1, "x", 1)
    r1, r3 = toward(r0, "y", 1), toward(r0, "y", -1)
    sums = gram(krylov_basis, hessian_product)
    l1, l7, sums = together(l1, l7, sums)
    l2, l6 = toward(l1, "z", 1), toward(l7, "z", -1)
    l2, l6, x2 = together(l2, l6, x2)
    l3, l5 = toward(l2, "z", 1), toward(l6, "z", -1)
    r2 = toward(r1, "y", 1)
    l4 = toward(l3, "z", 1)

    inputs = [x0, x1, x2, x3]
    near = [l0, l1, l2, l3, l5, l6, l7, r0, r1, r3]
    copy = pltpu.VMEM((ZS, YS * CHIP, WIDE), jnp.bfloat16)
    sums = project(near_kernel, place, inputs, basis, sums, near, SEQS, [copy])
    sums = project(far_kernel, place, inputs, basis, sums, [l4, r2], YS, [])
    sums = sum_everywhere(sums)

    rotation = jnp.pad(rotation, ((0, 128 - K), (0, 128 - TOP)))
    none = jnp.zeros((1,), jnp.float32)
    *results, little = finish(False, none, sums, rotation, krylov_basis, hessian_product)

    def measured(results):
        squares = squared_length(sums, krylov_basis, hessian_product)[None]
        return tuple(
            finish(True, squares, sums, rotation, krylov_basis, hessian_product)[:3]
        )

    new_vector, hessenberg, influence = lax.cond(
        little[0] == 1, measured, lambda results: tuple(results), results
    )
    return new_vector, hessenberg[0], influence


def solution(mesh):
    chips = jax.sharding.Mesh(mesh.devices.reshape(YS, ZS, 2, XS), ("y", "z", "core", "x"))
    col, tok = ("y", "z", "core"), "x"
    return jax.shard_map(
        on_device,
        mesh=chips,
        in_specs=(P(None, tok, col), P(tok, col), P(col, tok), P(tok, col), P()),
        out_specs=(P(tok, col), P(), P()),
        check_vma=False,
    )
```

```python
import functools

import jax
import jax.numpy as jnp
from jax import lax
from jax.experimental import pallas as pl
from jax.experimental.pallas import tpu as pltpu
from jax.sharding import PartitionSpec as P

LEN = 512
SEQS = 8
K = 8
TOP = 4
YS = 4
ZS = 8
XS = 4
CHIP = 128
WIDE = 512
GRAM = 16
DOTS = GRAM + K
SELF = DOTS + 1
PAIRS = [(k, l) for k in range(K) for l in range(k, K)]
HIGHEST = lax.Precision.HIGHEST
MB = 2**20


def toward(value, axis, sign):
    size = lax.axis_size(axis)
    axes = ("core", axis) if axis == "x" else (axis, "core")

    def place(i, core):
        return core * size + i if axis == "x" else i * 2 + core

    pairs = [
        (place(i, core), place((i + (sign if core == 0 else -sign)) % size, core))
        for i in range(size)
        for core in range(2)
    ]
    return lax.ppermute(value, axes, pairs)


def swap_core(value):
    return lax.ppermute(value, "core", [(0, 1), (1, 0)])


def together(*values):
    return lax.optimization_barrier(values)


def sum_over(value, axes):
    copies = jnp.broadcast_to(value[None], (lax.axis_size(axes),) + value.shape)
    return jnp.sum(lax.all_to_all(copies, axes, 0, 0), axis=0)


def sum_everywhere(value):
    return sum_over(sum_over(value, ("z", "core")), ("y", "x"))


def cells():
    shape = (8, 128)
    return (lax.broadcasted_iota(jnp.int32, shape, axis) for axis in range(2))


def total_of(value, axis=None):
    if axis is None:
        return total_of(total_of(value, 0), 1)
    return jnp.sum(value, axis=axis, keepdims=True)


def gram_kernel(basis_ref, field_ref, out_ref):
    count = len(PAIRS) + K + 1

    def step(at, totals):
        rows = pl.ds(pl.multiple_of(at * 16, 16), 16)
        stack = [basis_ref[k, rows, :].astype(jnp.float32) for k in range(K)]
        field = field_ref[rows, :]
        terms = [stack[k] * stack[l] for k, l in PAIRS] + [stack[k] * field for k in range(K)]
        terms.append(field * field)
        return tuple(t + (a[:8] + a[8:]) for t, a in zip(totals, terms))

    zero = jnp.zeros((8, 128), jnp.float32)
    totals = lax.fori_loop(0, field_ref.shape[0] // 16, step, (zero,) * count)
    totals = [total_of(total) for total in totals]
    row, lane = cells()
    out = jnp.where((row == 0) & (lane == SELF), totals[-1], 0.0)
    for (k, l), total in zip(PAIRS, totals):
        here = ((row == k) & (lane == GRAM + l)) | ((row == l) & (lane == GRAM + k))
        out = jnp.where(here, total, out)
    for k in range(K):
        out = jnp.where((row == k) & (lane == DOTS), totals[len(PAIRS) + k], out)
    out_ref[...] = out


def gram(basis, field):
    return pl.pallas_call(
        gram_kernel,
        out_shape=jax.ShapeDtypeStruct((8, 128), jnp.float32),
        in_specs=[pl.BlockSpec(memory_space=pltpu.VMEM)] * 2,
        out_specs=pl.BlockSpec(memory_space=pltpu.VMEM),
        compiler_params=pltpu.CompilerParams(vmem_limit_bytes=8 * MB),
        cost_estimate=pl.CostEstimate(flops=24 * MB, bytes_accessed=18 * MB, transcendentals=0),
        name="gram",
    )(basis, field)


def weigh(sums):
    row, lane = cells()
    overlaps = jnp.where((lane >= GRAM) & (lane < GRAM + K), sums, 0.0)

    def times(column):
        across = total_of(jnp.where(lane - GRAM == row, column, 0.0), 0)
        return total_of(overlaps * across, 1)

    first = total_of(jnp.where(lane == DOTS, sums, 0.0), 1)
    whole = total_of(jnp.where((lane == SELF) & (row == 0), sums, 0.0))
    weights = first + (first - times(first))
    squares = whole + total_of(weights * (times(weights) - (first + first)), 0)
    return weights, squares, whole


def spread(weights):
    return [jnp.broadcast_to(weights[k : k + 1], (16, 128)) for k in range(K)]


def take_off(weights, basis_ref, field_ref, rows):
    rest = field_ref[rows, :]
    for k in range(K):
        rest = rest - weights[k] * basis_ref[k, rows, :].astype(jnp.float32)
    return rest


def squares_kernel(sums_ref, basis_ref, field_ref, out_ref):
    weights = spread(weigh(sums_ref[...])[0])

    def step(at, total):
        rest = take_off(weights, basis_ref, field_ref, pl.ds(pl.multiple_of(at * 16, 16), 16))
        square = rest * rest
        return total + (square[:8] + square[8:])

    out_ref[...] = lax.fori_loop(
        0, field_ref.shape[0] // 16, step, jnp.zeros((8, 128), jnp.float32)
    )


def squared_length(sums, basis, field):
    vmem = pl.BlockSpec(memory_space=pltpu.VMEM)
    parts = pl.pallas_call(
        squares_kernel,
        out_shape=jax.ShapeDtypeStruct((8, 128), jnp.float32),
        in_specs=[vmem] * 3,
        out_specs=vmem,
        compiler_params=pltpu.CompilerParams(vmem_limit_bytes=8 * MB),
        name="squares",
    )(sums, basis, field)
    return jnp.sum(sum_everywhere(parts))


def finish_kernel(given, squares_ref, sums_ref, rotation_ref, basis_ref, field_ref, *out_refs):
    new_ref, hessenberg_ref, influence_ref, little_ref, spread_ref = out_refs

    @pl.when(pl.program_id(0) == 0)
    def _():
        sums = sums_ref[...]
        column, squares, whole = weigh(sums)
        little_ref[0] = (squares * 256.0 < whole).astype(jnp.int32)[0, 0]
        if given:
            squares = squares_ref[...]
        length = jnp.sqrt(squares + 1e-06)
        for k, weight in enumerate(spread(column)):
            spread_ref[k] = weight
        spread_ref[K] = jnp.broadcast_to(1.0 / length, (16, 128))
        row, lane = cells()
        across = total_of(jnp.where(lane == row, column, 0.0), 0)
        hessenberg_ref[...] = jnp.where(lane[:1] == K, length, across)[:, : K + 1]
        influence_ref[...] = lax.dot_general(
            rotation_ref[...],
            jnp.where(lane < K, sums, 0.0),
            (((1,), (1,)), ((), ())),
            precision=HIGHEST,
            preferred_element_type=jnp.float32,
        )[:TOP]

    weights = [spread_ref[k] for k in range(K)]
    scale = spread_ref[K]

    def step(at, carry):
        rows = pl.ds(pl.multiple_of(at * 16, 16), 16)
        rest = take_off(weights, basis_ref, field_ref, rows)
        new_ref[rows, :] = (rest * scale).astype(jnp.bfloat16)
        return carry

    lax.fori_loop(0, field_ref.shape[0] // 16, step, 0, unroll=4)


def finish(given, squares, sums, rotation, basis, field):
    vmem = pl.BlockSpec(memory_space=pltpu.VMEM)
    rows = field.shape[0] // 4
    block = pl.BlockSpec((rows, 128), lambda t: (t, 0))
    return pl.pallas_call(
        functools.partial(finish_kernel, given),
        out_shape=[
            jax.ShapeDtypeStruct(field.shape, jnp.bfloat16),
            jax.ShapeDtypeStruct((1, K + 1), jnp.float32),
            jax.ShapeDtypeStruct((TOP, SEQS), jnp.float32),
            jax.ShapeDtypeStruct((1,), jnp.int32),
        ],
        grid=(4,),
        in_specs=[vmem] * 3 + [pl.BlockSpec((K, rows, 128), lambda t: (0, t, 0)), block],
        out_specs=[block, vmem, vmem, pl.BlockSpec(memory_space=pltpu.SMEM)],
        scratch_shapes=[pltpu.VMEM((K + 1, 16, 128), jnp.float32)],
        compiler_params=pltpu.CompilerParams(vmem_limit_bytes=8 * MB),
        cost_estimate=pl.CostEstimate(flops=6 * MB, bytes_accessed=6 * MB, transcendentals=0),
        name="finish",
    )(squares, sums, rotation, basis, field)


def turn_basis_kernel(core_ref, own_ref, other_ref, left_ref, right_ref):
    for at, ref in enumerate((own_ref, other_ref)):
        turned = ref[0].T
        left_ref[0, at * 128 : (at + 1) * 128, :] = turned[:, :WIDE]
        right_ref[0, at * 128 : (at + 1) * 128, :] = turned[:, WIDE:]


def turn_basis(core, basis, other):
    half = other.shape[1] // 2
    return pl.pallas_call(
        turn_basis_kernel,
        out_shape=[jax.ShapeDtypeStruct((K, 256, WIDE), jnp.bfloat16)] * 2,
        grid_spec=pltpu.PrefetchScalarGridSpec(
            num_scalar_prefetch=1,
            grid=(K,),
            in_specs=[pl.BlockSpec((1, half, 128), lambda k, core: (k, core[0], 0))] * 2,
            out_specs=[pl.BlockSpec((1, 256, WIDE), lambda k, core: (k, 0, 0))] * 2,
        ),
        compiler_params=pltpu.CompilerParams(vmem_limit_bytes=8 * MB),
        cost_estimate=pl.CostEstimate(flops=0, bytes_accessed=8 * MB, transcendentals=0),
        name="turn_basis",
    )(core, basis, other)


def turn_inputs_kernel(core_ref, own_ref, other_ref, out_ref):
    for at, ref in enumerate((own_ref, other_ref)):
        parts = ref[...].reshape(-1, 2, CHIP // 2, 128)
        turned = jnp.concatenate([parts[:, 1:], parts[:, :1]], axis=1)
        parts = jnp.where(core_ref[0] == 1, turned, parts)
        out_ref[at * 128 : (at + 1) * 128, :] = parts.reshape(-1, 128).T


def turn_inputs(core, own, other):
    vmem = pl.BlockSpec(memory_space=pltpu.VMEM)
    return pl.pallas_call(
        turn_inputs_kernel,
        out_shape=jax.ShapeDtypeStruct((256, own.shape[0]), jnp.bfloat16),
        in_specs=[pl.BlockSpec(memory_space=pltpu.SMEM), vmem, vmem],
        out_specs=vmem,
        compiler_params=pltpu.CompilerParams(vmem_limit_bytes=8 * MB),
        cost_estimate=pl.CostEstimate(flops=0, bytes_accessed=MB, transcendentals=0),
        name="turn_inputs",
    )(core, own, other)


def keep_parts(parts_ref, slot, tile):
    high = tile.astype(jnp.bfloat16)
    parts_ref[2 * slot] = high
    parts_ref[2 * slot + 1] = (tile - high.astype(jnp.float32)).astype(jnp.bfloat16)


def products(parts_ref, count, basis_ref):
    cross = jnp.zeros((count * 64, 256), jnp.float32)
    for at in range(8):
        rows = slice(at * 32, (at + 1) * 32)
        tiles = parts_ref[: 2 * count, rows, :].reshape(count * 64, WIDE)
        basis = basis_ref[:, rows, :].reshape(256, WIDE)
        cross = cross + lax.dot_general(
            tiles, basis, (((1,), (1,)), ((), ())), preferred_element_type=jnp.float32
        )
    row = lax.broadcasted_iota(jnp.int32, cross.shape, 0)
    lane = lax.broadcasted_iota(jnp.int32, cross.shape, 1)
    cross = jnp.where(lax.rem(row, 32) == lax.rem(lane, 32), cross, 0.0)
    return jnp.sum(cross.reshape(count, 64, 256), axis=1)


def add_products(out_ref, sums, owners):
    owner = lax.broadcasted_iota(jnp.int32, (256, 128), 0) // 32
    pick = (owner == lax.broadcasted_iota(jnp.int32, (256, 128), 1)).astype(jnp.float32)
    sums = jnp.dot(sums, pick, precision=HIGHEST, preferred_element_type=jnp.float32)
    for at, owner in enumerate(owners):
        out_ref[pl.ds(owner, 1), :] += sums[at : at + 1]


class Place:
    def __init__(self, ref):
        self.y, self.z, self.x, self.sign = (ref[i] for i in range(4))

    def y_slot(self, y):
        return lax.rem(self.sign * (self.y - y) + 2 * YS, YS)

    def z_slot(self, z):
        return lax.rem(self.sign * (self.z - z) + 2 * ZS, ZS)

    def x_slot(self, x):
        return lax.rem(self.sign * (self.x - x) + 2 * XS, XS)

    def y_of(self, slot):
        return lax.rem(self.y - self.sign * slot + 2 * YS, YS)


def chip_rows(slot):
    return pl.ds(pl.multiple_of(slot * CHIP, CHIP), CHIP)


def example_tile(place, inputs_ref, y, part, block):
    grads = jnp.concatenate([block(place.z_slot(part * 4 + j)) for j in range(4)], axis=0)
    cols = pl.ds(pl.multiple_of(part * LEN, LEN), LEN)
    inputs = inputs_ref[place.x_slot(y), :, cols]
    return jnp.dot(inputs, grads, preferred_element_type=jnp.float32)


def rows_example(place, inputs_ref, parts_ref, at, slot_y, ref):
    y = place.y_of(slot_y)
    for part in range(2):
        tile = example_tile(place, inputs_ref, y, part, lambda d: ref[chip_rows(d), :])
        keep_parts(parts_ref, at + part, tile)
    return [y * 2, y * 2 + 1]


def fetch(pairs, sems):
    copies = [pltpu.make_async_copy(a, b, sems.at[at]) for at, (a, b) in enumerate(pairs)]
    for copy in copies:
        copy.start()
    return copies


def right_kernel(place_ref, far_basis_ref, before_ref, *refs):
    rights, out_ref, inputs_ref, parts_ref, basis_ref, right_ref, sems = refs[4:7], *refs[7:]
    pairs = [(ref, inputs_ref.at[slot]) for slot, ref in enumerate(refs[:4])]
    pairs += [(ref, right_ref.at[at]) for at, ref in enumerate(rights)]
    copies = fetch(pairs + [(far_basis_ref, basis_ref)], sems)
    inputs, copies, basis = copies[:4], copies[4:-1], copies[-1]
    place = Place(place_ref)
    out_ref[...] = before_ref[...]
    for copy in inputs:
        copy.wait()
    owners = []
    for at, slot_y in enumerate((0, 1, 3)):
        copies[at].wait()
        owners += rows_example(place, inputs_ref, parts_ref, 2 * at, slot_y, right_ref.at[at])
    basis.wait()
    add_products(out_ref, products(parts_ref, 6, basis_ref), owners)


def left_kernel(place_ref, far_basis_ref, before_ref, *refs):
    lefts, out_ref, inputs_ref, parts_ref, basis_ref, left_ref, sems = refs[4:11], *refs[11:]
    pairs = [(ref, inputs_ref.at[slot]) for slot, ref in enumerate(refs[:4])]
    pairs += [(ref, left_ref.at[slot]) for slot, ref in zip((0, 1, 2, 3, 5, 6, 7), lefts)]
    copies = fetch(pairs + [(far_basis_ref, basis_ref)], sems)
    place = Place(place_ref)
    out_ref[...] = before_ref[...]
    left_ref[4] = jnp.zeros_like(left_ref[4])
    for copy in copies[:-1]:
        copy.wait()
    for example in range(SEQS):
        y, part = example // 2, example % 2
        rows = chip_rows(place.y_slot(y))
        tile = example_tile(place, inputs_ref, y, part, lambda d: left_ref[d, rows, :])
        keep_parts(parts_ref, example, tile)
    copies[-1].wait()
    add_products(out_ref, products(parts_ref, SEQS, basis_ref), range(SEQS))


def far_kernel(place_ref, left_basis_ref, right_basis_ref, before_ref, *refs):
    left_ref, right_ref, out_ref, inputs_ref, parts_ref = refs[4:]
    place = Place(place_ref)
    out_ref[...] = before_ref[...]
    for slot in range(XS):
        inputs_ref[slot] = refs[slot][...]
    z = lax.rem(place.z + 4, ZS)
    owners = []
    for slot_y in range(YS):
        y = place.y_of(slot_y)
        tile = jnp.dot(
            inputs_ref[place.x_slot(y), :, chip_rows(z)],
            left_ref[slot_y * CHIP : (slot_y + 1) * CHIP, :],
            preferred_element_type=jnp.float32,
        )
        keep_parts(parts_ref, slot_y, tile)
        owners.append(y * 2 + z // 4)
    left = products(parts_ref, YS, left_basis_ref)
    owners += rows_example(place, inputs_ref, parts_ref, 0, 2, right_ref)
    right = products(parts_ref, 2, right_basis_ref)
    add_products(out_ref, jnp.concatenate([left, right]), owners)


def project(kernel, place, inputs, bases, before, grads, space, slots, scratch):
    vmem, large = pl.BlockSpec(memory_space=pltpu.VMEM), pl.BlockSpec(memory_space=space)
    return pl.pallas_call(
        kernel,
        out_shape=jax.ShapeDtypeStruct((8, 128), jnp.float32),
        in_specs=[pl.BlockSpec(memory_space=pltpu.SMEM)]
        + [large] * len(bases)
        + [vmem]
        + [large] * (len(inputs) + len(grads)),
        out_specs=vmem,
        scratch_shapes=[
            pltpu.VMEM((XS,) + inputs[0].shape, jnp.bfloat16),
            pltpu.VMEM((2 * slots, 256, WIDE), jnp.bfloat16),
        ]
        + scratch,
        compiler_params=pltpu.CompilerParams(vmem_limit_bytes=14 * MB),
        cost_estimate=pl.CostEstimate(
            flops=sum(512 * g.size for g in grads) + 512 * MB * slots,
            bytes_accessed=4 * MB,
            transcendentals=0,
        ),
        name=kernel.__name__,
    )(place, *bases, before, *inputs, *grads)


def on_device(krylov_basis, hessian_product, output_grads, layer_inputs, rotation):
    core = lax.axis_index("core")
    place = [lax.axis_index(axis) for axis in ("y", "z", "x")] + [1 - 2 * core]
    place = jnp.stack(place).astype(jnp.int32)
    core_id = core[None].astype(jnp.int32)
    half = krylov_basis.shape[1] // 2

    both = (output_grads, swap_core(output_grads))
    a, b = (
        jnp.concatenate(
            [lax.dynamic_slice_in_dim(g, core * half + at * WIDE, WIDE, 1) for g in both]
        )
        for at in range(2)
    )
    b1, b7 = toward(b, "z", 1), toward(b, "z", -1)
    a1, a3 = toward(a, "y", 1), toward(a, "y", -1)
    b1, b7, a1, a3, krylov, layer = together(b1, b7, a1, a3, krylov_basis, layer_inputs)
    x0 = turn_inputs(core_id, layer, swap_core(layer))
    x1, x3 = toward(x0, "x", 1), toward(x0, "x", -1)
    left_basis, right_basis = turn_basis(core_id, krylov, swap_core(krylov))
    b2, b6 = toward(b1, "z", 1), toward(b7, "z", -1)
    a2 = toward(a1, "y", 1)
    l0 = jnp.concatenate([a, a1, a2, a3])
    l0, field = together(l0, hessian_product)
    l1, l7 = toward(l0, "z", 1), toward(l0, "z", -1)
    b3, b5 = toward(b2, "z", 1), toward(b6, "z", -1)
    b4 = toward(b3, "z", 1)
    r0 = jnp.concatenate([b, b1, b2, b3, b4, b5, b6, b7])
    r1, r3 = toward(r0, "y", 1), toward(r0, "y", -1)
    sums = gram(krylov_basis, field)
    l1, l7, left_basis, right_basis = together(l1, l7, left_basis, right_basis)
    l2, l6 = toward(l1, "z", 1), toward(l7, "z", -1)
    x2 = toward(x1, "x", 1)
    l2, l6, sums = together(l2, l6, sums)
    l3, l5 = toward(l2, "z", 1), toward(l6, "z", -1)
    r2 = toward(r1, "y", 1)
    inputs = [x0, x1, x2, x3]
    sems = pltpu.SemaphoreType.DMA((12,))
    basis = pltpu.VMEM(left_basis.shape, jnp.bfloat16)
    held = [basis, pltpu.VMEM((3, ZS * CHIP, WIDE), jnp.bfloat16), sems]
    sums = project(
        right_kernel, place, inputs, [right_basis], sums, [r0, r1, r3], pl.ANY, 6, held
    )
    l3, l5, sums = together(l3, l5, sums)
    l4 = toward(l3, "z", 1)

    held = [basis, pltpu.VMEM((ZS, YS * CHIP, WIDE), jnp.bfloat16), sems]
    lefts = [l0, l1, l2, l3, l5, l6, l7]
    sums = project(left_kernel, place, inputs, [left_basis], sums, lefts, pl.ANY, SEQS, held)
    bases = [left_basis, right_basis]
    sums = project(far_kernel, place, inputs, bases, sums, [l4, r2], pltpu.VMEM, YS, [])
    rotation = jnp.pad(rotation.T, ((0, 8 - TOP), (0, 128 - K)))
    sums, rotation = together(sums, rotation)
    sums = sum_everywhere(sums)

    none = jnp.zeros((1, 1), jnp.float32)
    *results, little = finish(False, none, sums, rotation, krylov_basis, hessian_product)

    def measured(results):
        squares = squared_length(sums, krylov_basis, hessian_product)[None, None]
        return tuple(
            finish(True, squares, sums, rotation, krylov_basis, hessian_product)[:3]
        )

    new_vector, hessenberg, influence = lax.cond(
        little[0] == 1, measured, lambda results: tuple(results), results
    )
    return new_vector, hessenberg[0], influence.T


def solution(mesh):
    chips = jax.sharding.Mesh(mesh.devices.reshape(YS, ZS, 2, XS), ("y", "z", "core", "x"))
    col, tok = ("y", "z", "core"), "x"
    return jax.shard_map(
        on_device,
        mesh=chips,
        in_specs=(P(None, tok, col), P(tok, col), P(col, tok), P(tok, col), P()),
        out_specs=(P(tok, col), P(), P()),
        check_vma=False,
    )
```

```python
import functools

import jax
import jax.numpy as jnp
from jax import lax
from jax.experimental import pallas as pl
from jax.experimental.pallas import tpu as pltpu
from jax.sharding import PartitionSpec as P

LEN = 512
SEQS = 8
K = 8
TOP = 4
YS = 4
ZS = 8
XS = 4
CHIP = 128
WIDE = 512
GRAM = 16
DOTS = GRAM + K
SELF = DOTS + 1
HIGHEST = lax.Precision.HIGHEST
MB = 2**20


def toward(value, axis, sign):
    size = lax.axis_size(axis)
    axes = ("core", axis) if axis == "x" else (axis, "core")

    def place(i, core):
        return core * size + i if axis == "x" else i * 2 + core

    pairs = [
        (place(i, core), place((i + (sign if core == 0 else -sign)) % size, core))
        for i in range(size)
        for core in range(2)
    ]
    return lax.ppermute(value, axes, pairs)


def swap_core(value):
    return lax.ppermute(value, "core", [(0, 1), (1, 0)])


def together(*values):
    return lax.optimization_barrier(values)


def sum_over(value, axes):
    copies = jnp.broadcast_to(value[None], (lax.axis_size(axes),) + value.shape)
    return jnp.sum(lax.all_to_all(copies, axes, 0, 0), axis=0)


def sum_everywhere(value):
    return sum_over(sum_over(value, ("z", "core")), ("y", "x"))


def cells():
    shape = (8, 128)
    return (lax.broadcasted_iota(jnp.int32, shape, axis) for axis in range(2))


def total_of(value, axis=None):
    if axis is None:
        return total_of(total_of(value, 0), 1)
    return jnp.sum(value, axis=axis, keepdims=True)


def gram_kernel(basis_ref, field_ref, out_ref, cross_ref, dots_ref):
    at_step = pl.program_id(0)

    @pl.when(at_step == 0)
    def _():
        cross_ref[...] = jnp.zeros_like(cross_ref)
        dots_ref[...] = jnp.zeros_like(dots_ref)

    cross, dots = cross_ref[...], [dots_ref[k] for k in range(K + 1)]
    for at in range(0, field_ref.shape[0], 64):
        halves = [slice(at, at + 32), slice(at + 32, at + 64)]
        tile = jnp.concatenate([basis_ref[:, r, :].reshape(256, 128) for r in halves], axis=1)
        cross = cross + lax.dot_general(
            tile, tile, (((1,), (1,)), ((), ())), preferred_element_type=jnp.float32
        )
        for r in halves:
            field = field_ref[r, :]
            terms = [basis_ref[k, r, :].astype(jnp.float32) * field for k in range(K)]
            terms.append(field * field)
            dots = [d + (t[:8] + t[8:16]) + (t[16:24] + t[24:]) for d, t in zip(dots, terms)]
    cross_ref[...] = cross
    for k in range(K + 1):
        dots_ref[k] = dots[k]

    @pl.when(at_step == pl.num_programs(0) - 1)
    def _():
        out = matched(cross_ref[...], 8, GRAM)
        row, lane = cells()
        for k in range(K):
            out = jnp.where((row == k) & (lane == DOTS), total_of(dots_ref[k]), out)
        out_ref[...] = jnp.where((row == 0) & (lane == SELF), total_of(dots_ref[K]), out)


def gram(basis, field):
    rows = field.shape[0] // 4
    return pl.pallas_call(
        gram_kernel,
        out_shape=jax.ShapeDtypeStruct((8, 128), jnp.float32),
        grid=(4,),
        in_specs=[
            pl.BlockSpec((K, rows, 128), lambda t: (0, t, 0)),
            pl.BlockSpec((rows, 128), lambda t: (t, 0)),
        ],
        out_specs=pl.BlockSpec(memory_space=pltpu.VMEM),
        scratch_shapes=[
            pltpu.VMEM((256, 256), jnp.float32),
            pltpu.VMEM((K + 1, 8, 128), jnp.float32),
        ],
        compiler_params=pltpu.CompilerParams(vmem_limit_bytes=8 * MB),
        cost_estimate=pl.CostEstimate(flops=24 * MB, bytes_accessed=18 * MB, transcendentals=0),
        name="gram",
    )(basis, field)


def matched(cross, slots, lane):
    r = lax.broadcasted_iota(jnp.int32, cross.shape, 0)
    q = lax.broadcasted_iota(jnp.int32, cross.shape, 1)
    cross = jnp.where(lax.rem(r, 32) == lax.rem(q, 32), cross, 0.0)
    sums = jnp.sum(cross.reshape(slots, -1, 256), axis=1)
    return pick_lanes(sums, lane)


def pick_lanes(sums, lane):
    owner = lax.broadcasted_iota(jnp.int32, (256, 128), 0) // 32 + lane
    pick = (owner == lax.broadcasted_iota(jnp.int32, (256, 128), 1)).astype(jnp.float32)
    return jnp.dot(sums, pick, precision=HIGHEST, preferred_element_type=jnp.float32)


def weigh(sums):
    row, lane = cells()
    overlaps = jnp.where((lane >= GRAM) & (lane < GRAM + K), sums, 0.0)

    def times(column):
        across = total_of(jnp.where(lane - GRAM == row, column, 0.0), 0)
        return total_of(overlaps * across, 1)

    first = total_of(jnp.where(lane == DOTS, sums, 0.0), 1)
    whole = total_of(jnp.where((lane == SELF) & (row == 0), sums, 0.0))
    weights = first + (first - times(first))
    squares = whole + total_of(weights * (times(weights) - (first + first)), 0)
    return weights, squares, whole


def spread(weights):
    return [jnp.broadcast_to(weights[k : k + 1], (16, 128)) for k in range(K)]


def take_off(weights, basis_ref, field_ref, rows):
    rest = field_ref[rows, :]
    for k in range(K):
        rest = rest - weights[k] * basis_ref[k, rows, :].astype(jnp.float32)
    return rest


def squares_kernel(sums_ref, basis_ref, field_ref, out_ref):
    weights = spread(weigh(sums_ref[...])[0])

    def step(at, total):
        rest = take_off(weights, basis_ref, field_ref, pl.ds(pl.multiple_of(at * 16, 16), 16))
        square = rest * rest
        return total + (square[:8] + square[8:])

    out_ref[...] = lax.fori_loop(
        0, field_ref.shape[0] // 16, step, jnp.zeros((8, 128), jnp.float32)
    )


def squared_length(sums, basis, field):
    vmem = pl.BlockSpec(memory_space=pltpu.VMEM)
    parts = pl.pallas_call(
        squares_kernel,
        out_shape=jax.ShapeDtypeStruct((8, 128), jnp.float32),
        in_specs=[vmem] * 3,
        out_specs=vmem,
        compiler_params=pltpu.CompilerParams(vmem_limit_bytes=8 * MB),
        name="squares",
    )(sums, basis, field)
    return jnp.sum(sum_everywhere(parts))


def finish_kernel(given, squares_ref, sums_ref, rotation_ref, basis_ref, field_ref, *out_refs):
    new_ref, hessenberg_ref, influence_ref, little_ref, spread_ref = out_refs

    @pl.when(pl.program_id(0) == 0)
    def _():
        sums = sums_ref[...]
        column, squares, whole = weigh(sums)
        little_ref[0] = (squares * 256.0 < whole).astype(jnp.int32)[0, 0]
        if given:
            squares = squares_ref[...]
        length = jnp.sqrt(squares + 1e-06)
        for k, weight in enumerate(spread(column)):
            spread_ref[k] = weight
        spread_ref[K] = jnp.broadcast_to(1.0 / length, (16, 128))
        row, lane = cells()
        across = total_of(jnp.where(lane == row, column, 0.0), 0)
        hessenberg_ref[...] = jnp.where(lane[:1] == K, length, across)[:, : K + 1]
        influence_ref[...] = lax.dot_general(
            rotation_ref[...],
            jnp.where(lane < K, sums, 0.0),
            (((1,), (1,)), ((), ())),
            precision=HIGHEST,
            preferred_element_type=jnp.float32,
        )[:TOP]

    weights = [spread_ref[k] for k in range(K)]
    scale = spread_ref[K]

    def step(at, carry):
        rows = pl.ds(pl.multiple_of(at * 16, 16), 16)
        rest = take_off(weights, basis_ref, field_ref, rows)
        new_ref[rows, :] = (rest * scale).astype(jnp.bfloat16)
        return carry

    lax.fori_loop(0, field_ref.shape[0] // 16, step, 0, unroll=4)


def finish(given, squares, sums, rotation, basis, field):
    vmem = pl.BlockSpec(memory_space=pltpu.VMEM)
    rows = field.shape[0] // 4
    block = pl.BlockSpec((rows, 128), lambda t: (t, 0))
    return pl.pallas_call(
        functools.partial(finish_kernel, given),
        out_shape=[
            jax.ShapeDtypeStruct(field.shape, jnp.bfloat16),
            jax.ShapeDtypeStruct((1, K + 1), jnp.float32),
            jax.ShapeDtypeStruct((TOP, SEQS), jnp.float32),
            jax.ShapeDtypeStruct((1,), jnp.int32),
        ],
        grid=(4,),
        in_specs=[vmem] * 3 + [pl.BlockSpec((K, rows, 128), lambda t: (0, t, 0)), block],
        out_specs=[block, vmem, vmem, pl.BlockSpec(memory_space=pltpu.SMEM)],
        scratch_shapes=[pltpu.VMEM((K + 1, 16, 128), jnp.float32)],
        compiler_params=pltpu.CompilerParams(vmem_limit_bytes=8 * MB),
        cost_estimate=pl.CostEstimate(flops=6 * MB, bytes_accessed=6 * MB, transcendentals=0),
        name="finish",
    )(squares, sums, rotation, basis, field)


def turn_basis_kernel(core_ref, own_ref, other_ref, left_ref, right_ref):
    for k in range(2):
        for at, ref in enumerate((own_ref, other_ref)):
            turned = ref[k].T
            left_ref[k, at * 128 : (at + 1) * 128, :] = turned[:, :WIDE]
            right_ref[k, at * 128 : (at + 1) * 128, :] = turned[:, WIDE:]


def turn_basis(core, basis, other):
    half = other.shape[1] // 2
    return pl.pallas_call(
        turn_basis_kernel,
        out_shape=[jax.ShapeDtypeStruct((K, 256, WIDE), jnp.bfloat16)] * 2,
        grid_spec=pltpu.PrefetchScalarGridSpec(
            num_scalar_prefetch=1,
            grid=(K // 2,),
            in_specs=[pl.BlockSpec((2, half, 128), lambda k, core: (k, core[0], 0))] * 2,
            out_specs=[pl.BlockSpec((2, 256, WIDE), lambda k, core: (k, 0, 0))] * 2,
        ),
        compiler_params=pltpu.CompilerParams(vmem_limit_bytes=8 * MB),
        cost_estimate=pl.CostEstimate(flops=0, bytes_accessed=8 * MB, transcendentals=0),
        name="turn_basis",
    )(core, basis, other)


def turn_inputs_kernel(core_ref, own_ref, other_ref, out_ref):
    for at, ref in enumerate((own_ref, other_ref)):
        parts = ref[...].reshape(-1, 2, CHIP // 2, 128)
        turned = jnp.concatenate([parts[:, 1:], parts[:, :1]], axis=1)
        parts = jnp.where(core_ref[0] == 1, turned, parts)
        out_ref[at * 128 : (at + 1) * 128, :] = parts.reshape(-1, 128).T


def turn_inputs(core, own, other):
    vmem = pl.BlockSpec(memory_space=pltpu.VMEM)
    return pl.pallas_call(
        turn_inputs_kernel,
        out_shape=jax.ShapeDtypeStruct((256, own.shape[0]), jnp.bfloat16),
        in_specs=[pl.BlockSpec(memory_space=pltpu.SMEM), vmem, vmem],
        out_specs=vmem,
        compiler_params=pltpu.CompilerParams(vmem_limit_bytes=8 * MB),
        cost_estimate=pl.CostEstimate(flops=0, bytes_accessed=MB, transcendentals=0),
        name="turn_inputs",
    )(core, own, other)


def keep_parts(parts_ref, slot, tile):
    high = tile.astype(jnp.bfloat16)
    parts_ref[2 * slot] = high
    parts_ref[2 * slot + 1] = (tile - high.astype(jnp.float32)).astype(jnp.bfloat16)


def products(parts_ref, count, basis_ref):
    cross = jnp.zeros((count * 64, 256), jnp.float32)
    for at in range(8):
        rows = slice(at * 32, (at + 1) * 32)
        tiles = parts_ref[: 2 * count, rows, :].reshape(count * 64, WIDE)
        basis = basis_ref[:, rows, :].reshape(256, WIDE)
        cross = cross + lax.dot_general(
            tiles, basis, (((1,), (1,)), ((), ())), preferred_element_type=jnp.float32
        )
    row = lax.broadcasted_iota(jnp.int32, cross.shape, 0)
    lane = lax.broadcasted_iota(jnp.int32, cross.shape, 1)
    cross = jnp.where(lax.rem(row, 32) == lax.rem(lane, 32), cross, 0.0)
    return jnp.sum(cross.reshape(count, 64, 256), axis=1)


def add_products(out_ref, sums, owners):
    sums = pick_lanes(sums, 0)
    for at, owner in enumerate(owners):
        out_ref[pl.ds(owner, 1), :] += sums[at : at + 1]


class Place:
    def __init__(self, ref):
        self.y, self.z, self.x, self.sign = (ref[i] for i in range(4))

    def y_slot(self, y):
        return lax.rem(self.sign * (self.y - y) + 2 * YS, YS)

    def z_slot(self, z):
        return lax.rem(self.sign * (self.z - z) + 2 * ZS, ZS)

    def x_slot(self, x):
        return lax.rem(self.sign * (self.x - x) + 2 * XS, XS)

    def y_of(self, slot):
        return lax.rem(self.y - self.sign * slot + 2 * YS, YS)


def chip_rows(slot):
    return pl.ds(pl.multiple_of(slot * CHIP, CHIP), CHIP)


def example_tile(place, inputs_ref, y, part, block):
    grads = jnp.concatenate([block(place.z_slot(part * 4 + j)) for j in range(4)], axis=0)
    cols = pl.ds(pl.multiple_of(part * LEN, LEN), LEN)
    inputs = inputs_ref[place.x_slot(y), :, cols]
    return jnp.dot(inputs, grads, preferred_element_type=jnp.float32)


def rows_example(place, inputs_ref, parts_ref, at, slot_y, ref):
    y = place.y_of(slot_y)
    for part in range(2):
        tile = example_tile(place, inputs_ref, y, part, lambda d: ref[chip_rows(d), :])
        keep_parts(parts_ref, at + part, tile)
    return [y * 2, y * 2 + 1]


def fetch(pairs, sems):
    copies = [pltpu.make_async_copy(a, b, sems.at[at]) for at, (a, b) in enumerate(pairs)]
    for copy in copies:
        copy.start()
    return copies


def right_kernel(place_ref, far_basis_ref, before_ref, *refs):
    rights, out_ref, inputs_ref, parts_ref, basis_ref, right_ref, sems = refs[4:7], *refs[7:]
    pairs = [(ref, inputs_ref.at[slot]) for slot, ref in enumerate(refs[:4])]
    pairs += [(ref, right_ref.at[at]) for at, ref in enumerate(rights)]
    copies = fetch(pairs + [(far_basis_ref, basis_ref)], sems)
    inputs, copies, basis = copies[:4], copies[4:-1], copies[-1]
    place = Place(place_ref)
    out_ref[...] = before_ref[...]
    for copy in inputs:
        copy.wait()
    owners = []
    for at, slot_y in enumerate((0, 1, 3)):
        copies[at].wait()
        owners += rows_example(place, inputs_ref, parts_ref, 2 * at, slot_y, right_ref.at[at])
    basis.wait()
    add_products(out_ref, products(parts_ref, 6, basis_ref), owners)


def left_kernel(place_ref, far_basis_ref, before_ref, *refs):
    lefts, out_ref, inputs_ref, parts_ref, basis_ref, left_ref, sems = refs[4:11], *refs[11:]
    pairs = [(ref, inputs_ref.at[slot]) for slot, ref in enumerate(refs[:4])]
    pairs += [(ref, left_ref.at[slot]) for slot, ref in zip((0, 1, 2, 3, 5, 6, 7), lefts)]
    copies = fetch(pairs + [(far_basis_ref, basis_ref)], sems)
    place = Place(place_ref)
    out_ref[...] = before_ref[...]
    left_ref[4] = jnp.zeros_like(left_ref[4])
    for copy in copies[:-1]:
        copy.wait()
    for example in range(SEQS):
        y, part = example // 2, example % 2
        rows = chip_rows(place.y_slot(y))
        tile = example_tile(place, inputs_ref, y, part, lambda d: left_ref[d, rows, :])
        keep_parts(parts_ref, example, tile)
    copies[-1].wait()
    add_products(out_ref, products(parts_ref, SEQS, basis_ref), range(SEQS))


def far_kernel(place_ref, left_basis_ref, right_basis_ref, before_ref, *refs):
    left_ref, right_ref, out_ref, inputs_ref, parts_ref = refs[4:]
    place = Place(place_ref)
    out_ref[...] = before_ref[...]
    for slot in range(XS):
        inputs_ref[slot] = refs[slot][...]
    z = lax.rem(place.z + 4, ZS)
    owners = []
    for slot_y in range(YS):
        y = place.y_of(slot_y)
        tile = jnp.dot(
            inputs_ref[place.x_slot(y), :, chip_rows(z)],
            left_ref[slot_y * CHIP : (slot_y + 1) * CHIP, :],
            preferred_element_type=jnp.float32,
        )
        keep_parts(parts_ref, slot_y, tile)
        owners.append(y * 2 + z // 4)
    left = products(parts_ref, YS, left_basis_ref)
    owners += rows_example(place, inputs_ref, parts_ref, 0, 2, right_ref)
    right = products(parts_ref, 2, right_basis_ref)
    add_products(out_ref, jnp.concatenate([left, right]), owners)


def project(kernel, place, inputs, bases, before, grads, space, slots, scratch):
    vmem, large = pl.BlockSpec(memory_space=pltpu.VMEM), pl.BlockSpec(memory_space=space)
    return pl.pallas_call(
        kernel,
        out_shape=jax.ShapeDtypeStruct((8, 128), jnp.float32),
        in_specs=[pl.BlockSpec(memory_space=pltpu.SMEM)]
        + [large] * len(bases)
        + [vmem]
        + [large] * (len(inputs) + len(grads)),
        out_specs=vmem,
        scratch_shapes=[
            pltpu.VMEM((XS,) + inputs[0].shape, jnp.bfloat16),
            pltpu.VMEM((2 * slots, 256, WIDE), jnp.bfloat16),
        ]
        + scratch,
        compiler_params=pltpu.CompilerParams(vmem_limit_bytes=14 * MB),
        cost_estimate=pl.CostEstimate(
            flops=sum(512 * g.size for g in grads) + 512 * MB * slots,
            bytes_accessed=4 * MB,
            transcendentals=0,
        ),
        name=kernel.__name__,
    )(place, *bases, before, *inputs, *grads)


def on_device(krylov_basis, hessian_product, output_grads, layer_inputs, rotation):
    core = lax.axis_index("core")
    place = [lax.axis_index(axis) for axis in ("y", "z", "x")] + [1 - 2 * core]
    place = jnp.stack(place).astype(jnp.int32)
    core_id = core[None].astype(jnp.int32)
    half = krylov_basis.shape[1] // 2

    both = (output_grads, swap_core(output_grads))
    a, b = (
        jnp.concatenate(
            [lax.dynamic_slice_in_dim(g, core * half + at * WIDE, WIDE, 1) for g in both]
        )
        for at in range(2)
    )
    b1, b7 = toward(b, "z", 1), toward(b, "z", -1)
    a1, a3 = toward(a, "y", 1), toward(a, "y", -1)
    b1, b7, a1, a3, krylov, layer = together(b1, b7, a1, a3, krylov_basis, layer_inputs)
    x0 = turn_inputs(core_id, layer, swap_core(layer))
    x1, x3 = toward(x0, "x", 1), toward(x0, "x", -1)
    left_basis, right_basis = turn_basis(core_id, krylov, swap_core(krylov))
    b2, b6 = toward(b1, "z", 1), toward(b7, "z", -1)
    a2 = toward(a1, "y", 1)
    l0 = jnp.concatenate([a, a1, a2, a3])
    l0, field = together(l0, hessian_product)
    l1, l7 = toward(l0, "z", 1), toward(l0, "z", -1)
    b3, b5 = toward(b2, "z", 1), toward(b6, "z", -1)
    b4 = toward(b3, "z", 1)
    b4, left_basis, right_basis = together(b4, left_basis, right_basis)
    r0 = jnp.concatenate([b, b1, b2, b3, b4, b5, b6, b7])
    r1, r3 = toward(r0, "y", 1), toward(r0, "y", -1)
    sums = gram(krylov_basis, field)
    l1, l7 = together(l1, l7)
    l2, l6 = toward(l1, "z", 1), toward(l7, "z", -1)
    x2 = toward(x1, "x", 1)
    l2, l6, sums = together(l2, l6, sums)
    l3, l5 = toward(l2, "z", 1), toward(l6, "z", -1)
    r2 = toward(r1, "y", 1)
    inputs = [x0, x1, x2, x3]
    sems = pltpu.SemaphoreType.DMA((12,))
    basis = pltpu.VMEM(left_basis.shape, jnp.bfloat16)
    held = [basis, pltpu.VMEM((3, ZS * CHIP, WIDE), jnp.bfloat16), sems]
    sums = project(
        right_kernel, place, inputs, [right_basis], sums, [r0, r1, r3], pl.ANY, 6, held
    )
    l3, l5, sums = together(l3, l5, sums)
    l4 = toward(l3, "z", 1)

    held = [basis, pltpu.VMEM((ZS, YS * CHIP, WIDE), jnp.bfloat16), sems]
    lefts = [l0, l1, l2, l3, l5, l6, l7]
    sums = project(left_kernel, place, inputs, [left_basis], sums, lefts, pl.ANY, SEQS, held)
    bases = [left_basis, right_basis]
    sums = project(far_kernel, place, inputs, bases, sums, [l4, r2], pltpu.VMEM, YS, [])
    rotation = jnp.pad(rotation.T, ((0, 8 - TOP), (0, 128 - K)))
    sums, rotation = together(sums, rotation)
    sums = sum_everywhere(sums)

    none = jnp.zeros((1, 1), jnp.float32)
    *results, little = finish(False, none, sums, rotation, krylov_basis, hessian_product)

    def measured(results):
        squares = squared_length(sums, krylov_basis, hessian_product)[None, None]
        return tuple(
            finish(True, squares, sums, rotation, krylov_basis, hessian_product)[:3]
        )

    new_vector, hessenberg, influence = lax.cond(
        little[0] == 1, measured, lambda results: tuple(results), results
    )
    return new_vector, hessenberg[0], influence.T


def solution(mesh):
    chips = jax.sharding.Mesh(mesh.devices.reshape(YS, ZS, 2, XS), ("y", "z", "core", "x"))
    col, tok = ("y", "z", "core"), "x"
    return jax.shard_map(
        on_device,
        mesh=chips,
        in_specs=(P(None, tok, col), P(tok, col), P(col, tok), P(tok, col), P()),
        out_specs=(P(tok, col), P(), P()),
        check_vma=False,
    )
```

```python
import functools

import jax
import jax.numpy as jnp
from jax import lax
from jax.experimental import pallas as pl
from jax.experimental.pallas import tpu as pltpu
from jax.sharding import PartitionSpec as P

LEN = 512
SEQS = 8
K = 8
TOP = 4
YS = 4
ZS = 8
XS = 4
CHIP = 128
WIDE = 512
GRAM = 16
DOTS = GRAM + K
SELF = DOTS + 1
HIGHEST = lax.Precision.HIGHEST
MB = 2**20


def toward(value, axis, sign):
    size = lax.axis_size(axis)
    axes = ("core", axis) if axis == "x" else (axis, "core")

    def place(i, core):
        return core * size + i if axis == "x" else i * 2 + core

    pairs = [
        (place(i, core), place((i + (sign if core == 0 else -sign)) % size, core))
        for i in range(size)
        for core in range(2)
    ]
    return lax.ppermute(value, axes, pairs)


def swap_core(value):
    return lax.ppermute(value, "core", [(0, 1), (1, 0)])


def together(*values):
    return lax.optimization_barrier(values)


def sum_over(value, axes):
    copies = jnp.broadcast_to(value[None], (lax.axis_size(axes),) + value.shape)
    return jnp.sum(lax.all_to_all(copies, axes, 0, 0), axis=0)


def sum_everywhere(value):
    return sum_over(sum_over(value, ("z", "core")), ("y", "x"))


def cells():
    shape = (8, 128)
    return (lax.broadcasted_iota(jnp.int32, shape, axis) for axis in range(2))


def total_of(value, axis=None):
    if axis is None:
        return total_of(total_of(value, 0), 1)
    return jnp.sum(value, axis=axis, keepdims=True)


def gram_kernel(before_ref, basis_ref, field_ref, out_ref, cross_ref, dots_ref):
    at_step = pl.program_id(0)

    @pl.when(at_step == 0)
    def _():
        cross_ref[...] = jnp.zeros_like(cross_ref)
        dots_ref[...] = jnp.zeros_like(dots_ref)

    cross, dots = cross_ref[...], [dots_ref[k] for k in range(K + 1)]
    for at in range(0, field_ref.shape[0], 64):
        halves = [slice(at, at + 32), slice(at + 32, at + 64)]
        tile = jnp.concatenate([basis_ref[:, r, :].reshape(256, 128) for r in halves], axis=1)
        cross = cross + lax.dot_general(
            tile, tile, (((1,), (1,)), ((), ())), preferred_element_type=jnp.float32
        )
        for r in halves:
            field = field_ref[r, :]
            terms = [basis_ref[k, r, :].astype(jnp.float32) * field for k in range(K)]
            terms.append(field * field)
            dots = [d + (t[:8] + t[8:16]) + (t[16:24] + t[24:]) for d, t in zip(dots, terms)]
    cross_ref[...] = cross
    for k in range(K + 1):
        dots_ref[k] = dots[k]

    @pl.when(at_step == pl.num_programs(0) - 1)
    def _():
        out = matched(cross_ref[...], 8, GRAM)
        row, lane = cells()
        for k in range(K):
            out = jnp.where((row == k) & (lane == DOTS), total_of(dots_ref[k]), out)
        out = jnp.where((row == 0) & (lane == SELF), total_of(dots_ref[K]), out)
        out_ref[...] = before_ref[...] + out


def gram(before, basis, field):
    rows = field.shape[0] // 4
    return pl.pallas_call(
        gram_kernel,
        out_shape=jax.ShapeDtypeStruct((8, 128), jnp.float32),
        grid=(4,),
        in_specs=[
            pl.BlockSpec(memory_space=pltpu.VMEM),
            pl.BlockSpec((K, rows, 128), lambda t: (0, t, 0)),
            pl.BlockSpec((rows, 128), lambda t: (t, 0)),
        ],
        out_specs=pl.BlockSpec(memory_space=pltpu.VMEM),
        scratch_shapes=[
            pltpu.VMEM((256, 256), jnp.float32),
            pltpu.VMEM((K + 1, 8, 128), jnp.float32),
        ],
        compiler_params=pltpu.CompilerParams(vmem_limit_bytes=8 * MB),
        cost_estimate=pl.CostEstimate(flops=24 * MB, bytes_accessed=18 * MB, transcendentals=0),
        name="gram",
    )(before, basis, field)


def matched(cross, slots, lane):
    r = lax.broadcasted_iota(jnp.int32, cross.shape, 0)
    q = lax.broadcasted_iota(jnp.int32, cross.shape, 1)
    cross = jnp.where(lax.rem(r, 32) == lax.rem(q, 32), cross, 0.0)
    sums = jnp.sum(cross.reshape(slots, -1, 256), axis=1)
    return pick_lanes(sums, lane)


def pick_lanes(sums, lane):
    owner = lax.broadcasted_iota(jnp.int32, (256, 128), 0) // 32 + lane
    pick = (owner == lax.broadcasted_iota(jnp.int32, (256, 128), 1)).astype(jnp.float32)
    return jnp.dot(sums, pick, precision=HIGHEST, preferred_element_type=jnp.float32)


def weigh(sums):
    row, lane = cells()
    overlaps = jnp.where((lane >= GRAM) & (lane < GRAM + K), sums, 0.0)

    def times(column):
        across = total_of(jnp.where(lane - GRAM == row, column, 0.0), 0)
        return total_of(overlaps * across, 1)

    first = total_of(jnp.where(lane == DOTS, sums, 0.0), 1)
    whole = total_of(jnp.where((lane == SELF) & (row == 0), sums, 0.0))
    weights = first + (first - times(first))
    squares = whole + total_of(weights * (times(weights) - (first + first)), 0)
    return weights, squares, whole


def spread(weights):
    return [jnp.broadcast_to(weights[k : k + 1], (16, 128)) for k in range(K)]


def take_off(weights, basis_ref, field_ref, rows):
    rest = field_ref[rows, :]
    for k in range(K):
        rest = rest - weights[k] * basis_ref[k, rows, :].astype(jnp.float32)
    return rest


def squares_kernel(sums_ref, basis_ref, field_ref, out_ref):
    weights = spread(weigh(sums_ref[...])[0])

    def step(at, total):
        rest = take_off(weights, basis_ref, field_ref, pl.ds(pl.multiple_of(at * 16, 16), 16))
        square = rest * rest
        return total + (square[:8] + square[8:])

    out_ref[...] = lax.fori_loop(
        0, field_ref.shape[0] // 16, step, jnp.zeros((8, 128), jnp.float32)
    )


def squared_length(sums, basis, field):
    vmem = pl.BlockSpec(memory_space=pltpu.VMEM)
    parts = pl.pallas_call(
        squares_kernel,
        out_shape=jax.ShapeDtypeStruct((8, 128), jnp.float32),
        in_specs=[vmem] * 3,
        out_specs=vmem,
        compiler_params=pltpu.CompilerParams(vmem_limit_bytes=8 * MB),
        name="squares",
    )(sums, basis, field)
    return jnp.sum(sum_everywhere(parts))


def finish_kernel(given, squares_ref, sums_ref, rotation_ref, far_basis_ref, far_field_ref, *refs):
    new_ref, hessenberg_ref, influence_ref, little_ref, basis_ref, field_ref, sems = refs
    quarters = [slice(at, at + 512) for at in range(0, field_ref.shape[0], 512)]
    pairs = []
    for part in quarters:
        pairs.append((far_basis_ref.at[:, part], basis_ref.at[:, part]))
        pairs.append((far_field_ref.at[part], field_ref.at[part]))
    copies = fetch(pairs, sems)
    sums = sums_ref[...]
    column, squares, whole = weigh(sums)
    little_ref[0] = (squares * 256.0 < whole).astype(jnp.int32)[0, 0]
    if given:
        squares = squares_ref[...]
    length = jnp.sqrt(squares + 1e-06)
    weights = spread(column)
    scale = jnp.broadcast_to(1.0 / length, (16, 128))
    row, lane = cells()
    across = total_of(jnp.where(lane == row, column, 0.0), 0)
    hessenberg_ref[...] = jnp.where(lane[:1] == K, length, across)[:, : K + 1]
    influence_ref[...] = lax.dot_general(
        rotation_ref[...],
        jnp.where(lane < K, sums, 0.0),
        (((1,), (1,)), ((), ())),
        precision=HIGHEST,
        preferred_element_type=jnp.float32,
    )[:TOP]
    for at, part in enumerate(quarters):
        copies[2 * at].wait()
        copies[2 * at + 1].wait()

        def step(i, carry):
            rows = pl.ds(pl.multiple_of(part.start + i * 16, 16), 16)
            rest = take_off(weights, basis_ref, field_ref, rows)
            new_ref[rows, :] = (rest * scale).astype(jnp.bfloat16)
            return carry

        lax.fori_loop(0, 32, step, 0, unroll=4)


def finish(given, squares, sums, rotation, basis, field):
    vmem, anywhere = (pl.BlockSpec(memory_space=m) for m in (pltpu.VMEM, pl.ANY))
    return pl.pallas_call(
        functools.partial(finish_kernel, given),
        out_shape=[
            jax.ShapeDtypeStruct(field.shape, jnp.bfloat16),
            jax.ShapeDtypeStruct((1, K + 1), jnp.float32),
            jax.ShapeDtypeStruct((TOP, SEQS), jnp.float32),
            jax.ShapeDtypeStruct((1,), jnp.int32),
        ],
        in_specs=[vmem] * 3 + [anywhere] * 2,
        out_specs=[vmem] * 3 + [pl.BlockSpec(memory_space=pltpu.SMEM)],
        scratch_shapes=[
            pltpu.VMEM(basis.shape, jnp.bfloat16),
            pltpu.VMEM(field.shape, jnp.float32),
            pltpu.SemaphoreType.DMA((8,)),
        ],
        compiler_params=pltpu.CompilerParams(vmem_limit_bytes=8 * MB),
        cost_estimate=pl.CostEstimate(flops=6 * MB, bytes_accessed=6 * MB, transcendentals=0),
        name="finish",
    )(squares, sums, rotation, basis, field)


def turn_basis_kernel(core_ref, own_ref, other_ref, left_ref, right_ref):
    for k in range(2):
        for at, ref in enumerate((own_ref, other_ref)):
            turned = ref[k].T
            left_ref[k, at * 128 : (at + 1) * 128, :] = turned[:, :WIDE]
            right_ref[k, at * 128 : (at + 1) * 128, :] = turned[:, WIDE:]


def turn_basis(core, basis, other):
    half = other.shape[1] // 2
    return pl.pallas_call(
        turn_basis_kernel,
        out_shape=[jax.ShapeDtypeStruct((K, 256, WIDE), jnp.bfloat16)] * 2,
        grid_spec=pltpu.PrefetchScalarGridSpec(
            num_scalar_prefetch=1,
            grid=(K // 2,),
            in_specs=[pl.BlockSpec((2, half, 128), lambda k, core: (k, core[0], 0))] * 2,
            out_specs=[pl.BlockSpec((2, 256, WIDE), lambda k, core: (k, 0, 0))] * 2,
        ),
        compiler_params=pltpu.CompilerParams(vmem_limit_bytes=8 * MB),
        cost_estimate=pl.CostEstimate(flops=0, bytes_accessed=8 * MB, transcendentals=0),
        name="turn_basis",
    )(core, basis, other)


def turn_inputs_kernel(core_ref, own_ref, other_ref, out_ref):
    for at, ref in enumerate((own_ref, other_ref)):
        parts = ref[...].reshape(-1, 2, CHIP // 2, 128)
        turned = jnp.concatenate([parts[:, 1:], parts[:, :1]], axis=1)
        parts = jnp.where(core_ref[0] == 1, turned, parts)
        out_ref[at * 128 : (at + 1) * 128, :] = parts.reshape(-1, 128).T


def turn_inputs(core, own, other):
    vmem = pl.BlockSpec(memory_space=pltpu.VMEM)
    return pl.pallas_call(
        turn_inputs_kernel,
        out_shape=jax.ShapeDtypeStruct((256, own.shape[0]), jnp.bfloat16),
        in_specs=[pl.BlockSpec(memory_space=pltpu.SMEM), vmem, vmem],
        out_specs=vmem,
        compiler_params=pltpu.CompilerParams(vmem_limit_bytes=8 * MB),
        cost_estimate=pl.CostEstimate(flops=0, bytes_accessed=MB, transcendentals=0),
        name="turn_inputs",
    )(core, own, other)


def keep_parts(parts_ref, slot, tile):
    high = tile.astype(jnp.bfloat16)
    parts_ref[2 * slot] = high
    parts_ref[2 * slot + 1] = (tile - high.astype(jnp.float32)).astype(jnp.bfloat16)


def products(parts_ref, count, basis_ref):
    cross = jnp.zeros((count * 64, 256), jnp.float32)
    for at in range(8):
        rows = slice(at * 32, (at + 1) * 32)
        tiles = parts_ref[: 2 * count, rows, :].reshape(count * 64, WIDE)
        basis = basis_ref[:, rows, :].reshape(256, WIDE)
        cross = cross + lax.dot_general(
            tiles, basis, (((1,), (1,)), ((), ())), preferred_element_type=jnp.float32
        )
    row = lax.broadcasted_iota(jnp.int32, cross.shape, 0)
    lane = lax.broadcasted_iota(jnp.int32, cross.shape, 1)
    cross = jnp.where(lax.rem(row, 32) == lax.rem(lane, 32), cross, 0.0)
    return jnp.sum(cross.reshape(count, 64, 256), axis=1)


def add_products(out_ref, sums, owners):
    sums = pick_lanes(sums, 0)
    for at, owner in enumerate(owners):
        out_ref[pl.ds(owner, 1), :] += sums[at : at + 1]


class Place:
    def __init__(self, ref):
        self.y, self.z, self.x, self.sign = (ref[i] for i in range(4))

    def y_slot(self, y):
        return lax.rem(self.sign * (self.y - y) + 2 * YS, YS)

    def z_slot(self, z):
        return lax.rem(self.sign * (self.z - z) + 2 * ZS, ZS)

    def x_slot(self, x):
        return lax.rem(self.sign * (self.x - x) + 2 * XS, XS)

    def y_of(self, slot):
        return lax.rem(self.y - self.sign * slot + 2 * YS, YS)


def chip_rows(slot):
    return pl.ds(pl.multiple_of(slot * CHIP, CHIP), CHIP)


def example_tile(place, inputs_ref, y, part, block):
    grads = jnp.concatenate([block(place.z_slot(part * 4 + j)) for j in range(4)], axis=0)
    cols = pl.ds(pl.multiple_of(part * LEN, LEN), LEN)
    inputs = inputs_ref[place.x_slot(y), :, cols]
    return jnp.dot(inputs, grads, preferred_element_type=jnp.float32)


def rows_example(place, inputs_ref, parts_ref, at, slot_y, ref):
    y = place.y_of(slot_y)
    for part in range(2):
        tile = example_tile(place, inputs_ref, y, part, lambda d: ref[chip_rows(d), :])
        keep_parts(parts_ref, at + part, tile)
    return [y * 2, y * 2 + 1]


def fetch(pairs, sems):
    copies = [pltpu.make_async_copy(a, b, sems.at[at]) for at, (a, b) in enumerate(pairs)]
    for copy in copies:
        copy.start()
    return copies


def right_kernel(place_ref, far_basis_ref, before_ref, *refs):
    rights, out_ref, inputs_ref, parts_ref, basis_ref, right_ref, sems = refs[4:7], *refs[7:]
    pairs = [(ref, inputs_ref.at[slot]) for slot, ref in enumerate(refs[:4])]
    pairs += [(ref, right_ref.at[at]) for at, ref in enumerate(rights)]
    copies = fetch(pairs + [(far_basis_ref, basis_ref)], sems)
    inputs, copies, basis = copies[:4], copies[4:-1], copies[-1]
    place = Place(place_ref)
    out_ref[...] = before_ref[...]
    for copy in inputs:
        copy.wait()
    owners = []
    for at, slot_y in enumerate((0, 1, 3)):
        copies[at].wait()
        owners += rows_example(place, inputs_ref, parts_ref, 2 * at, slot_y, right_ref.at[at])
    basis.wait()
    add_products(out_ref, products(parts_ref, 6, basis_ref), owners)


def left_kernel(place_ref, far_basis_ref, before_ref, *refs):
    lefts, out_ref, inputs_ref, parts_ref, basis_ref, left_ref, sems = refs[4:11], *refs[11:]
    pairs = [(ref, inputs_ref.at[slot]) for slot, ref in enumerate(refs[:4])]
    pairs += [(ref, left_ref.at[slot]) for slot, ref in zip((0, 1, 2, 3, 5, 6, 7), lefts)]
    copies = fetch(pairs + [(far_basis_ref, basis_ref)], sems)
    place = Place(place_ref)
    out_ref[...] = before_ref[...]
    left_ref[4] = jnp.zeros_like(left_ref[4])
    for copy in copies[:-1]:
        copy.wait()
    for example in range(SEQS):
        y, part = example // 2, example % 2
        rows = chip_rows(place.y_slot(y))
        tile = example_tile(place, inputs_ref, y, part, lambda d: left_ref[d, rows, :])
        keep_parts(parts_ref, example, tile)
    copies[-1].wait()
    add_products(out_ref, products(parts_ref, SEQS, basis_ref), range(SEQS))


def far_kernel(place_ref, left_basis_ref, right_basis_ref, before_ref, *refs):
    left_ref, right_ref, out_ref, inputs_ref, parts_ref = refs[4:]
    place = Place(place_ref)
    out_ref[...] = before_ref[...]
    for slot in range(XS):
        inputs_ref[slot] = refs[slot][...]
    z = lax.rem(place.z + 4, ZS)
    owners = []
    for slot_y in range(YS):
        y = place.y_of(slot_y)
        tile = jnp.dot(
            inputs_ref[place.x_slot(y), :, chip_rows(z)],
            left_ref[slot_y * CHIP : (slot_y + 1) * CHIP, :],
            preferred_element_type=jnp.float32,
        )
        keep_parts(parts_ref, slot_y, tile)
        owners.append(y * 2 + z // 4)
    left = products(parts_ref, YS, left_basis_ref)
    owners += rows_example(place, inputs_ref, parts_ref, 0, 2, right_ref)
    right = products(parts_ref, 2, right_basis_ref)
    add_products(out_ref, jnp.concatenate([left, right]), owners)


def project(kernel, place, inputs, bases, before, grads, space, slots, scratch):
    vmem, large = pl.BlockSpec(memory_space=pltpu.VMEM), pl.BlockSpec(memory_space=space)
    return pl.pallas_call(
        kernel,
        out_shape=jax.ShapeDtypeStruct((8, 128), jnp.float32),
        in_specs=[pl.BlockSpec(memory_space=pltpu.SMEM)]
        + [large] * len(bases)
        + [vmem]
        + [large] * (len(inputs) + len(grads)),
        out_specs=vmem,
        scratch_shapes=[
            pltpu.VMEM((XS,) + inputs[0].shape, jnp.bfloat16),
            pltpu.VMEM((2 * slots, 256, WIDE), jnp.bfloat16),
        ]
        + scratch,
        compiler_params=pltpu.CompilerParams(vmem_limit_bytes=14 * MB),
        cost_estimate=pl.CostEstimate(
            flops=sum(512 * g.size for g in grads) + 512 * MB * slots,
            bytes_accessed=4 * MB,
            transcendentals=0,
        ),
        name=kernel.__name__,
    )(place, *bases, before, *inputs, *grads)


def on_device(krylov_basis, hessian_product, output_grads, layer_inputs, rotation):
    core = lax.axis_index("core")
    place = [lax.axis_index(axis) for axis in ("y", "z", "x")] + [1 - 2 * core]
    place = jnp.stack(place).astype(jnp.int32)
    core_id = core[None].astype(jnp.int32)
    half = krylov_basis.shape[1] // 2

    both = (output_grads, swap_core(output_grads))
    a, b = (
        jnp.concatenate(
            [lax.dynamic_slice_in_dim(g, core * half + at * WIDE, WIDE, 1) for g in both]
        )
        for at in range(2)
    )
    b1, b7 = toward(b, "z", 1), toward(b, "z", -1)
    a1, a3 = toward(a, "y", 1), toward(a, "y", -1)
    b1, b7, a1, a3, krylov = together(b1, b7, a1, a3, krylov_basis)
    b2, b6 = toward(b1, "z", 1), toward(b7, "z", -1)
    a2 = toward(a1, "y", 1)
    l0 = jnp.concatenate([a, a1, a2, a3])
    l0, layer = together(l0, layer_inputs)
    x0 = turn_inputs(core_id, layer, swap_core(layer))
    x1, x3 = toward(x0, "x", 1), toward(x0, "x", -1)
    left_basis, right_basis = turn_basis(core_id, krylov, swap_core(krylov))
    l1, l7 = toward(l0, "z", 1), toward(l0, "z", -1)
    b3, b5 = toward(b2, "z", 1), toward(b6, "z", -1)
    b4 = toward(b3, "z", 1)
    b4, left_basis, right_basis = together(b4, left_basis, right_basis)
    r0 = jnp.concatenate([b, b1, b2, b3, b4, b5, b6, b7])
    r1, r3 = toward(r0, "y", 1), toward(r0, "y", -1)
    l1, l7 = together(l1, l7)
    l2, l6 = toward(l1, "z", 1), toward(l7, "z", -1)
    x2 = toward(x1, "x", 1)
    l2, l6 = together(l2, l6)
    l3, l5 = toward(l2, "z", 1), toward(l6, "z", -1)
    r2 = toward(r1, "y", 1)
    inputs = [x0, x1, x2, x3]
    sems = pltpu.SemaphoreType.DMA((12,))
    basis = pltpu.VMEM(left_basis.shape, jnp.bfloat16)
    held = [basis, pltpu.VMEM((3, ZS * CHIP, WIDE), jnp.bfloat16), sems]
    sums = jnp.zeros((8, 128), jnp.float32)
    sums = project(
        right_kernel, place, inputs, [right_basis], sums, [r0, r1, r3], pl.ANY, 6, held
    )
    l3, l5, sums = together(l3, l5, sums)
    l4 = toward(l3, "z", 1)

    held = [basis, pltpu.VMEM((ZS, YS * CHIP, WIDE), jnp.bfloat16), sems]
    lefts = [l0, l1, l2, l3, l5, l6, l7]
    sums = project(left_kernel, place, inputs, [left_basis], sums, lefts, pl.ANY, SEQS, held)
    sums = gram(sums, krylov_basis, hessian_product)
    bases = [left_basis, right_basis]
    sums = project(far_kernel, place, inputs, bases, sums, [l4, r2], pltpu.VMEM, YS, [])
    rotation = jnp.pad(rotation.T, ((0, 8 - TOP), (0, 128 - K)))
    sums, rotation = together(sums, rotation)
    sums = sum_everywhere(sums)

    none = jnp.zeros((1, 1), jnp.float32)
    *results, little = finish(False, none, sums, rotation, krylov_basis, hessian_product)

    def measured(results):
        squares = squared_length(sums, krylov_basis, hessian_product)[None, None]
        return tuple(
            finish(True, squares, sums, rotation, krylov_basis, hessian_product)[:3]
        )

    new_vector, hessenberg, influence = lax.cond(
        little[0] == 1, measured, lambda results: tuple(results), results
    )
    return new_vector, hessenberg[0], influence.T


def solution(mesh):
    chips = jax.sharding.Mesh(mesh.devices.reshape(YS, ZS, 2, XS), ("y", "z", "core", "x"))
    col, tok = ("y", "z", "core"), "x"
    return jax.shard_map(
        on_device,
        mesh=chips,
        in_specs=(P(None, tok, col), P(tok, col), P(col, tok), P(tok, col), P()),
        out_specs=(P(tok, col), P(), P()),
        check_vma=False,
    )
```

```python
import functools

import jax
import jax.numpy as jnp
from jax import lax
from jax.experimental import pallas as pl
from jax.experimental.pallas import tpu as pltpu
from jax.sharding import PartitionSpec as P

LEN = 512
SEQS = 8
K = 8
TOP = 4
YS = 4
ZS = 8
XS = 4
CHIP = 128
WIDE = 512
GRAM = 16
DOTS = GRAM + K
SELF = DOTS + 1
HIGHEST = lax.Precision.HIGHEST
MB = 2**20


def toward(value, axis, sign):
    size = lax.axis_size(axis)
    axes = ("core", axis) if axis == "x" else (axis, "core")

    def place(i, core):
        return core * size + i if axis == "x" else i * 2 + core

    pairs = [
        (place(i, core), place((i + (sign if core == 0 else -sign)) % size, core))
        for i in range(size)
        for core in range(2)
    ]
    return lax.ppermute(value, axes, pairs)


def swap_core(value):
    return lax.ppermute(value, "core", [(0, 1), (1, 0)])


def together(*values):
    return lax.optimization_barrier(values)


def sum_over(value, axes):
    copies = jnp.broadcast_to(value[None], (lax.axis_size(axes),) + value.shape)
    return jnp.sum(lax.all_to_all(copies, axes, 0, 0), axis=0)


def sum_everywhere(value):
    return sum_over(sum_over(value, ("z", "core")), ("y", "x"))


def cells():
    shape = (8, 128)
    return (lax.broadcasted_iota(jnp.int32, shape, axis) for axis in range(2))


def total_of(value, axis=None):
    if axis is None:
        return total_of(total_of(value, 0), 1)
    return jnp.sum(value, axis=axis, keepdims=True)


def gram_kernel(before_ref, basis_ref, field_ref, out_ref, cross_ref, dots_ref):
    at_step = pl.program_id(0)

    @pl.when(at_step == 0)
    def _():
        cross_ref[...] = jnp.zeros_like(cross_ref)
        dots_ref[...] = jnp.zeros_like(dots_ref)

    cross, dots = cross_ref[...], [dots_ref[k] for k in range(K + 1)]
    for at in range(0, field_ref.shape[0], 64):
        halves = [slice(at, at + 32), slice(at + 32, at + 64)]
        tile = jnp.concatenate([basis_ref[:, r, :].reshape(256, 128) for r in halves], axis=1)
        cross = cross + lax.dot_general(
            tile, tile, (((1,), (1,)), ((), ())), preferred_element_type=jnp.float32
        )
        for r in halves:
            field = field_ref[r, :]
            terms = [basis_ref[k, r, :].astype(jnp.float32) * field for k in range(K)]
            terms.append(field * field)
            dots = [d + (t[:8] + t[8:16]) + (t[16:24] + t[24:]) for d, t in zip(dots, terms)]
    cross_ref[...] = cross
    for k in range(K + 1):
        dots_ref[k] = dots[k]

    @pl.when(at_step == pl.num_programs(0) - 1)
    def _():
        out = matched(cross_ref[...], 8, GRAM)
        row, lane = cells()
        for k in range(K):
            out = jnp.where((row == k) & (lane == DOTS), total_of(dots_ref[k]), out)
        out = jnp.where((row == 0) & (lane == SELF), total_of(dots_ref[K]), out)
        out_ref[...] = before_ref[...] + out


def gram(before, basis, field):
    rows = field.shape[0] // 4
    return pl.pallas_call(
        gram_kernel,
        out_shape=jax.ShapeDtypeStruct((8, 128), jnp.float32),
        grid=(4,),
        in_specs=[
            pl.BlockSpec(memory_space=pltpu.VMEM),
            pl.BlockSpec((K, rows, 128), lambda t: (0, t, 0)),
            pl.BlockSpec((rows, 128), lambda t: (t, 0)),
        ],
        out_specs=pl.BlockSpec(memory_space=pltpu.VMEM),
        scratch_shapes=[
            pltpu.VMEM((256, 256), jnp.float32),
            pltpu.VMEM((K + 1, 8, 128), jnp.float32),
        ],
        compiler_params=pltpu.CompilerParams(vmem_limit_bytes=8 * MB),
        cost_estimate=pl.CostEstimate(flops=24 * MB, bytes_accessed=18 * MB, transcendentals=0),
        name="gram",
    )(before, basis, field)


def matched(cross, slots, lane):
    r = lax.broadcasted_iota(jnp.int32, cross.shape, 0)
    q = lax.broadcasted_iota(jnp.int32, cross.shape, 1)
    cross = jnp.where(lax.rem(r, 32) == lax.rem(q, 32), cross, 0.0)
    sums = jnp.sum(cross.reshape(slots, -1, 256), axis=1)
    return pick_lanes(sums, lane)


def pick_lanes(sums, lane):
    owner = lax.broadcasted_iota(jnp.int32, (256, 128), 0) // 32 + lane
    pick = (owner == lax.broadcasted_iota(jnp.int32, (256, 128), 1)).astype(jnp.float32)
    return jnp.dot(sums, pick, precision=HIGHEST, preferred_element_type=jnp.float32)


def weigh(sums):
    row, lane = cells()
    overlaps = jnp.where((lane >= GRAM) & (lane < GRAM + K), sums, 0.0)

    def times(column):
        across = total_of(jnp.where(lane - GRAM == row, column, 0.0), 0)
        return total_of(overlaps * across, 1)

    first = total_of(jnp.where(lane == DOTS, sums, 0.0), 1)
    whole = total_of(jnp.where((lane == SELF) & (row == 0), sums, 0.0))
    weights = first + (first - times(first))
    squares = whole + total_of(weights * (times(weights) - (first + first)), 0)
    return weights, squares, whole


def spread(weights):
    return [jnp.broadcast_to(weights[k : k + 1], (16, 128)) for k in range(K)]


def take_off(weights, basis_ref, field_ref, rows):
    rest = field_ref[rows, :]
    for k in range(K):
        rest = rest - weights[k] * basis_ref[k, rows, :].astype(jnp.float32)
    return rest


def squares_kernel(sums_ref, basis_ref, field_ref, out_ref):
    weights = spread(weigh(sums_ref[...])[0])

    def step(at, total):
        rest = take_off(weights, basis_ref, field_ref, pl.ds(pl.multiple_of(at * 16, 16), 16))
        square = rest * rest
        return total + (square[:8] + square[8:])

    out_ref[...] = lax.fori_loop(
        0, field_ref.shape[0] // 16, step, jnp.zeros((8, 128), jnp.float32)
    )


def squared_length(sums, basis, field):
    vmem = pl.BlockSpec(memory_space=pltpu.VMEM)
    parts = pl.pallas_call(
        squares_kernel,
        out_shape=jax.ShapeDtypeStruct((8, 128), jnp.float32),
        in_specs=[vmem] * 3,
        out_specs=vmem,
        compiler_params=pltpu.CompilerParams(vmem_limit_bytes=8 * MB),
        name="squares",
    )(sums, basis, field)
    return jnp.sum(sum_everywhere(parts))


def finish_kernel(given, squares_ref, sums_ref, rotation_ref, far_basis_ref, far_field_ref, *refs):
    new_ref, hessenberg_ref, influence_ref, little_ref, basis_ref, field_ref, sems = refs
    quarters = [slice(at, at + 512) for at in range(0, field_ref.shape[0], 512)]
    pairs = []
    for part in quarters:
        pairs.append((far_basis_ref.at[:, part], basis_ref.at[:, part]))
        pairs.append((far_field_ref.at[part], field_ref.at[part]))
    copies = fetch(pairs, sems)
    sums = sums_ref[...]
    column, squares, whole = weigh(sums)
    little_ref[0] = (squares * 256.0 < whole).astype(jnp.int32)[0, 0]
    if given:
        squares = squares_ref[...]
    length = jnp.sqrt(squares + 1e-06)
    weights = spread(column)
    scale = jnp.broadcast_to(1.0 / length, (16, 128))
    row, lane = cells()
    across = total_of(jnp.where(lane == row, column, 0.0), 0)
    hessenberg_ref[...] = jnp.where(lane[:1] == K, length, across)[:, : K + 1]
    influence_ref[...] = lax.dot_general(
        rotation_ref[...],
        jnp.where(lane < K, sums, 0.0),
        (((1,), (1,)), ((), ())),
        precision=HIGHEST,
        preferred_element_type=jnp.float32,
    )[:TOP]
    for at, part in enumerate(quarters):
        copies[2 * at].wait()
        copies[2 * at + 1].wait()

        def step(i, carry):
            rows = pl.ds(pl.multiple_of(part.start + i * 16, 16), 16)
            rest = take_off(weights, basis_ref, field_ref, rows)
            new_ref[rows, :] = (rest * scale).astype(jnp.bfloat16)
            return carry

        lax.fori_loop(0, 32, step, 0, unroll=4)


def finish(given, squares, sums, rotation, basis, field):
    vmem, anywhere = (pl.BlockSpec(memory_space=m) for m in (pltpu.VMEM, pl.ANY))
    return pl.pallas_call(
        functools.partial(finish_kernel, given),
        out_shape=[
            jax.ShapeDtypeStruct(field.shape, jnp.bfloat16),
            jax.ShapeDtypeStruct((1, K + 1), jnp.float32),
            jax.ShapeDtypeStruct((TOP, SEQS), jnp.float32),
            jax.ShapeDtypeStruct((1,), jnp.int32),
        ],
        in_specs=[vmem] * 3 + [anywhere] * 2,
        out_specs=[vmem] * 3 + [pl.BlockSpec(memory_space=pltpu.SMEM)],
        scratch_shapes=[
            pltpu.VMEM(basis.shape, jnp.bfloat16),
            pltpu.VMEM(field.shape, jnp.float32),
            pltpu.SemaphoreType.DMA((8,)),
        ],
        compiler_params=pltpu.CompilerParams(vmem_limit_bytes=8 * MB),
        cost_estimate=pl.CostEstimate(flops=6 * MB, bytes_accessed=6 * MB, transcendentals=0),
        name="finish",
    )(squares, sums, rotation, basis, field)


def turn_basis_kernel(core_ref, own_ref, other_ref, left_ref, right_ref):
    for k in range(2):
        for at, ref in enumerate((own_ref, other_ref)):
            turned = ref[k].T
            left_ref[k, at * 128 : (at + 1) * 128, :] = turned[:, :WIDE]
            right_ref[k, at * 128 : (at + 1) * 128, :] = turned[:, WIDE:]


def turn_basis(core, basis, other):
    half = other.shape[1] // 2
    return pl.pallas_call(
        turn_basis_kernel,
        out_shape=[jax.ShapeDtypeStruct((K, 256, WIDE), jnp.bfloat16)] * 2,
        grid_spec=pltpu.PrefetchScalarGridSpec(
            num_scalar_prefetch=1,
            grid=(K // 2,),
            in_specs=[pl.BlockSpec((2, half, 128), lambda k, core: (k, core[0], 0))] * 2,
            out_specs=[pl.BlockSpec((2, 256, WIDE), lambda k, core: (k, 0, 0))] * 2,
        ),
        compiler_params=pltpu.CompilerParams(vmem_limit_bytes=8 * MB),
        cost_estimate=pl.CostEstimate(flops=0, bytes_accessed=8 * MB, transcendentals=0),
        name="turn_basis",
    )(core, basis, other)


def turn_inputs_kernel(core_ref, own_ref, other_ref, out_ref):
    for at, ref in enumerate((own_ref, other_ref)):
        parts = ref[...].reshape(-1, 2, CHIP // 2, 128)
        turned = jnp.concatenate([parts[:, 1:], parts[:, :1]], axis=1)
        parts = jnp.where(core_ref[0] == 1, turned, parts)
        out_ref[at * 128 : (at + 1) * 128, :] = parts.reshape(-1, 128).T


def turn_inputs(core, own, other):
    vmem = pl.BlockSpec(memory_space=pltpu.VMEM)
    return pl.pallas_call(
        turn_inputs_kernel,
        out_shape=jax.ShapeDtypeStruct((256, own.shape[0]), jnp.bfloat16),
        in_specs=[pl.BlockSpec(memory_space=pltpu.SMEM), vmem, vmem],
        out_specs=vmem,
        compiler_params=pltpu.CompilerParams(vmem_limit_bytes=8 * MB),
        cost_estimate=pl.CostEstimate(flops=0, bytes_accessed=MB, transcendentals=0),
        name="turn_inputs",
    )(core, own, other)


def keep_parts(parts_ref, slot, tile):
    high = tile.astype(jnp.bfloat16)
    parts_ref[2 * slot] = high
    parts_ref[2 * slot + 1] = (tile - high.astype(jnp.float32)).astype(jnp.bfloat16)


def products(parts_ref, count, basis_ref):
    cross = jnp.zeros((count * 64, 256), jnp.float32)
    for at in range(8):
        rows = slice(at * 32, (at + 1) * 32)
        tiles = parts_ref[: 2 * count, rows, :].reshape(count * 64, WIDE)
        basis = basis_ref[:, rows, :].reshape(256, WIDE)
        cross = cross + lax.dot_general(
            tiles, basis, (((1,), (1,)), ((), ())), preferred_element_type=jnp.float32
        )
    row = lax.broadcasted_iota(jnp.int32, cross.shape, 0)
    lane = lax.broadcasted_iota(jnp.int32, cross.shape, 1)
    cross = jnp.where(lax.rem(row, 32) == lax.rem(lane, 32), cross, 0.0)
    return jnp.sum(cross.reshape(count, 64, 256), axis=1)


def add_products(out_ref, sums, owners):
    sums = pick_lanes(sums, 0)
    for at, owner in enumerate(owners):
        out_ref[pl.ds(owner, 1), :] += sums[at : at + 1]


class Place:
    def __init__(self, ref):
        self.y, self.z, self.x, self.sign = (ref[i] for i in range(4))

    def y_slot(self, y):
        return lax.rem(self.sign * (self.y - y) + 2 * YS, YS)

    def z_slot(self, z):
        return lax.rem(self.sign * (self.z - z) + 2 * ZS, ZS)

    def x_slot(self, x):
        return lax.rem(self.sign * (self.x - x) + 2 * XS, XS)

    def y_of(self, slot):
        return lax.rem(self.y - self.sign * slot + 2 * YS, YS)


def chip_rows(slot):
    return pl.ds(pl.multiple_of(slot * CHIP, CHIP), CHIP)


def example_tile(place, inputs_ref, y, part, block):
    grads = jnp.concatenate([block(place.z_slot(part * 4 + j)) for j in range(4)], axis=0)
    cols = pl.ds(pl.multiple_of(part * LEN, LEN), LEN)
    inputs = inputs_ref[place.x_slot(y), :, cols]
    return jnp.dot(inputs, grads, preferred_element_type=jnp.float32)


def rows_example(place, inputs_ref, parts_ref, at, slot_y, ref):
    y = place.y_of(slot_y)
    for part in range(2):
        tile = example_tile(place, inputs_ref, y, part, lambda d: ref[chip_rows(d), :])
        keep_parts(parts_ref, at + part, tile)
    return [y * 2, y * 2 + 1]


def fetch(pairs, sems):
    copies = [pltpu.make_async_copy(a, b, sems.at[at]) for at, (a, b) in enumerate(pairs)]
    for copy in copies:
        copy.start()
    return copies


def right_kernel(place_ref, far_basis_ref, before_ref, *refs):
    rights, out_ref, inputs_ref, parts_ref, basis_ref, right_ref, sems = refs[4:7], *refs[7:]
    pairs = [(ref, inputs_ref.at[slot]) for slot, ref in enumerate(refs[:4])]
    pairs += [(ref, right_ref.at[at]) for at, ref in enumerate(rights)]
    copies = fetch(pairs + [(far_basis_ref, basis_ref)], sems)
    inputs, copies, basis = copies[:4], copies[4:-1], copies[-1]
    place = Place(place_ref)
    out_ref[...] = before_ref[...]
    for copy in inputs:
        copy.wait()
    owners = []
    for at, slot_y in enumerate((0, 1, 3)):
        copies[at].wait()
        owners += rows_example(place, inputs_ref, parts_ref, 2 * at, slot_y, right_ref.at[at])
    basis.wait()
    add_products(out_ref, products(parts_ref, 6, basis_ref), owners)


def left_kernel(place_ref, far_basis_ref, before_ref, *refs):
    lefts, out_ref, inputs_ref, parts_ref, basis_ref, left_ref, sems = refs[4:11], *refs[11:]
    pairs = [(ref, inputs_ref.at[slot]) for slot, ref in enumerate(refs[:4])]
    pairs += [(ref, left_ref.at[slot]) for slot, ref in zip((0, 1, 2, 3, 5, 6, 7), lefts)]
    copies = fetch(pairs + [(far_basis_ref, basis_ref)], sems)
    place = Place(place_ref)
    out_ref[...] = before_ref[...]
    left_ref[4] = jnp.zeros_like(left_ref[4])
    for copy in copies[:-1]:
        copy.wait()
    for example in range(SEQS):
        y, part = example // 2, example % 2
        rows = chip_rows(place.y_slot(y))
        tile = example_tile(place, inputs_ref, y, part, lambda d: left_ref[d, rows, :])
        keep_parts(parts_ref, example, tile)
    copies[-1].wait()
    add_products(out_ref, products(parts_ref, SEQS, basis_ref), range(SEQS))


def far_kernel(place_ref, left_basis_ref, right_basis_ref, before_ref, *refs):
    left_ref, right_ref, out_ref, inputs_ref, parts_ref = refs[4:]
    place = Place(place_ref)
    out_ref[...] = before_ref[...]
    for slot in range(XS):
        inputs_ref[slot] = refs[slot][...]
    z = lax.rem(place.z + 4, ZS)
    owners = []
    for slot_y in range(YS):
        y = place.y_of(slot_y)
        tile = jnp.dot(
            inputs_ref[place.x_slot(y), :, chip_rows(z)],
            left_ref[slot_y * CHIP : (slot_y + 1) * CHIP, :],
            preferred_element_type=jnp.float32,
        )
        keep_parts(parts_ref, slot_y, tile)
        owners.append(y * 2 + z // 4)
    left = products(parts_ref, YS, left_basis_ref)
    owners += rows_example(place, inputs_ref, parts_ref, 0, 2, right_ref)
    right = products(parts_ref, 2, right_basis_ref)
    add_products(out_ref, jnp.concatenate([left, right]), owners)


def project(kernel, place, inputs, bases, before, grads, space, slots, scratch):
    vmem, large = pl.BlockSpec(memory_space=pltpu.VMEM), pl.BlockSpec(memory_space=space)
    return pl.pallas_call(
        kernel,
        out_shape=jax.ShapeDtypeStruct((8, 128), jnp.float32),
        in_specs=[pl.BlockSpec(memory_space=pltpu.SMEM)]
        + [large] * len(bases)
        + [vmem]
        + [large] * (len(inputs) + len(grads)),
        out_specs=vmem,
        scratch_shapes=[
            pltpu.VMEM((XS,) + inputs[0].shape, jnp.bfloat16),
            pltpu.VMEM((2 * slots, 256, WIDE), jnp.bfloat16),
        ]
        + scratch,
        compiler_params=pltpu.CompilerParams(vmem_limit_bytes=14 * MB),
        cost_estimate=pl.CostEstimate(
            flops=sum(512 * g.size for g in grads) + 512 * MB * slots,
            bytes_accessed=4 * MB,
            transcendentals=0,
        ),
        name=kernel.__name__,
    )(place, *bases, before, *inputs, *grads)


def on_device(krylov_basis, hessian_product, output_grads, layer_inputs, rotation):
    core = lax.axis_index("core")
    place = [lax.axis_index(axis) for axis in ("y", "z", "x")] + [1 - 2 * core]
    place = jnp.stack(place).astype(jnp.int32)
    core_id = core[None].astype(jnp.int32)
    half = krylov_basis.shape[1] // 2

    both = (output_grads, swap_core(output_grads))
    a, b = (
        jnp.concatenate(
            [lax.dynamic_slice_in_dim(g, core * half + at * WIDE, WIDE, 1) for g in both]
        )
        for at in range(2)
    )
    b1, b7 = toward(b, "z", 1), toward(b, "z", -1)
    a1, a3 = toward(a, "y", 1), toward(a, "y", -1)
    b1, b7, a1, a3, krylov = together(b1, b7, a1, a3, krylov_basis)
    b2, b6 = toward(b1, "z", 1), toward(b7, "z", -1)
    a2 = toward(a1, "y", 1)
    l0 = jnp.concatenate([a, a1, a2, a3])
    l0, layer = together(l0, layer_inputs)
    x0 = turn_inputs(core_id, layer, swap_core(layer))
    x1, x3 = toward(x0, "x", 1), toward(x0, "x", -1)
    left_basis, right_basis = turn_basis(core_id, krylov, swap_core(krylov))
    l1, l7 = toward(l0, "z", 1), toward(l0, "z", -1)
    b3, b5 = toward(b2, "z", 1), toward(b6, "z", -1)
    b4 = toward(b3, "z", 1)
    b4, left_basis, right_basis = together(b4, left_basis, right_basis)
    r0 = jnp.concatenate([b, b1, b2, b3, b4, b5, b6, b7])
    r1, r3 = toward(r0, "y", 1), toward(r0, "y", -1)
    l1, l7, x3 = together(l1, l7, x3)
    l2, l6 = toward(l1, "z", 1), toward(l7, "z", -1)
    x2 = toward(x1, "x", 1)
    l2, l6 = together(l2, l6)
    l3, l5 = toward(l2, "z", 1), toward(l6, "z", -1)
    r2 = toward(r1, "y", 1)
    inputs = [x0, x1, x2, x3]
    sems = pltpu.SemaphoreType.DMA((12,))
    basis = pltpu.VMEM(left_basis.shape, jnp.bfloat16)
    held = [basis, pltpu.VMEM((3, ZS * CHIP, WIDE), jnp.bfloat16), sems]
    sums = jnp.zeros((8, 128), jnp.float32)
    sums = project(
        right_kernel, place, inputs, [right_basis], sums, [r0, r1, r3], pl.ANY, 6, held
    )
    l3, l5, sums = together(l3, l5, sums)
    l4 = toward(l3, "z", 1)

    held = [basis, pltpu.VMEM((ZS, YS * CHIP, WIDE), jnp.bfloat16), sems]
    lefts = [l0, l1, l2, l3, l5, l6, l7]
    sums = project(left_kernel, place, inputs, [left_basis], sums, lefts, pl.ANY, SEQS, held)
    sums = gram(sums, krylov_basis, hessian_product)
    bases = [left_basis, right_basis]
    sums = project(far_kernel, place, inputs, bases, sums, [l4, r2], pltpu.VMEM, YS, [])
    rotation = jnp.pad(rotation.T, ((0, 8 - TOP), (0, 128 - K)))
    sums, rotation = together(sums, rotation)
    sums = sum_everywhere(sums)

    none = jnp.zeros((1, 1), jnp.float32)
    *results, little = finish(False, none, sums, rotation, krylov_basis, hessian_product)

    def measured(results):
        squares = squared_length(sums, krylov_basis, hessian_product)[None, None]
        return tuple(
            finish(True, squares, sums, rotation, krylov_basis, hessian_product)[:3]
        )

    new_vector, hessenberg, influence = lax.cond(
        little[0] == 1, measured, lambda results: tuple(results), results
    )
    return new_vector, hessenberg[0], influence.T


def solution(mesh):
    chips = jax.sharding.Mesh(mesh.devices.reshape(YS, ZS, 2, XS), ("y", "z", "core", "x"))
    col, tok = ("y", "z", "core"), "x"
    return jax.shard_map(
        on_device,
        mesh=chips,
        in_specs=(P(None, tok, col), P(tok, col), P(col, tok), P(tok, col), P()),
        out_specs=(P(tok, col), P(), P()),
        check_vma=False,
    )
```
